256 devices in a mesh: pair: 2 (over core), seq: 32 (over y, z), tensor: 4 (over x).
Axes of the slice: x: 4, y: 4, z: 8, core: 2. Of those that a mesh axis runs over, the one named last changes fastest.
Arguments:
- latents: bfloat16 [2, 1, 8192, 1152], P('pair', None, 'seq'), may hold values from -36 to 36
- noise: bfloat16 [2, 1, 8192, 1152], P('pair', None, 'seq'), may hold values from -4 to 4
- timesteps: int32 [2, 1], P('pair'), may hold values from 50 to 949
- ref_losses: float32 [2, 1], replicated, may hold values from 0.5 to 2.5
- weights: bfloat16 [1152, 2, 4, 1152], P(None, None, None, 'tensor'), may hold values from -2.7 to 2.7
Outputs:
- dpo_loss: float32 [], replicated
- weight_grads: float32 [1152, 2, 4, 1152], P(('pair', 'seq'), None, None, 'tensor')
The draws below stay inside these ranges and needn't reach their ends.
All inputs are finite; a program needn't handle non-finite values.
Results may differ from the reference program's by a relative error of at most 0.02.
Values may be sent and summed in bfloat16 or wider, within the bound.
A program may use at most 128 MiB of HBM per device.

```python
import math
import jax
import jax.numpy as jnp
from jax import lax

D = 1152
HEADS = 16
POSITIONS = 256
BATCH = 1
HEAD_DIM = 72
FRAMES = 32
TOKENS = 8192


def draw_latents(key, part):
    key = jax.random.fold_in(key, 11)
    base_key = jax.random.fold_in(key, 0)
    frame_pos = (jnp.arange(TOKENS) // POSITIONS).astype(jnp.float32)
    ramp = 3.0 ** (frame_pos / max(FRAMES - 1, 1))
    values = jax.random.truncated_normal(base_key, -4.0, 4.0, (2, BATCH, TOKENS, D), jnp.float32)
    return (values * ramp[None, None, :, None]).astype(jnp.bfloat16)


def draw_weights(key, part):
    key = jax.random.fold_in(key, 23)
    base_key = jax.random.fold_in(key, 0)
    values = jax.random.truncated_normal(base_key, -4.0, 4.0, (D, 2, 4, D), jnp.float32) * D ** (-0.5)
    return values.astype(jnp.bfloat16)


def levels(key, dims, cuts, least, high):
    gain = 1.0
    for position, shards_of in cuts:
        heights = jax.random.uniform(jax.random.fold_in(jax.random.fold_in(key, 6), position), (shards_of,), jnp.float32, least / len(cuts), high / len(cuts))
        gain = gain * jnp.repeat(jnp.exp(heights), dims[position] // shards_of).reshape((-1,) + (1,) * (len(dims) - 1 - position))
    return gain


def normal_values(rng, dims, deviation, most, shards=(), dtype=jnp.bfloat16):
    gain = levels(rng, dims, shards, -0.22, 0.18) if shards else 1.0
    values = jax.random.normal(rng, dims, jnp.float32) * deviation * gain
    return jnp.minimum(jnp.maximum(values, -most), most).astype(dtype)


def setup_inputs(seed: int = 0) -> dict:
    streams_of = jax.random.split(jax.random.key(seed), 6)
    return {
        "latents": draw_latents(jax.random.fold_in(streams_of[5], 71), 0),
        "noise": normal_values(streams_of[1], (2, BATCH, TOKENS, D), 1.0, 4.0, ((0, 2), (2, 32))),
        "timesteps": jax.random.randint(streams_of[2], (2, BATCH), 50, 950).astype(jnp.int32),
        "ref_losses": jnp.clip(jax.random.uniform(streams_of[3], (2, BATCH), jnp.float32, 0.5, 2.5), 0.5, 2.5),
        "weights": draw_weights(jax.random.fold_in(streams_of[5], 71), 0),
    }


beta_dpo = 0.5
norm_eps = 1e-06

def layer_norm(hidden):
    center = hidden - lax.optimization_barrier(jnp.mean(hidden, axis=-1, keepdims=True))
    inv_std = lax.rsqrt(lax.optimization_barrier(jnp.mean(center * center, axis=-1, keepdims=True)) + norm_eps)
    return (center * inv_std, inv_std)

def norm_backward(grad_norm, normed, inv_std):
    mean_grad = lax.optimization_barrier(jnp.mean(grad_norm, axis=-1, keepdims=True))
    mean_prod = lax.optimization_barrier(jnp.mean(grad_norm * normed, axis=-1, keepdims=True))
    return inv_std * (grad_norm - mean_grad - normed * mean_prod)

def attend_forward(queries, keyset, valueset):
    factor = HEAD_DIM ** (-0.5)
    scores = jnp.einsum('bqhc,bkhc->bhqk', queries.astype(jnp.float32), keyset.astype(jnp.float32)) * factor
    soft_weights = jax.nn.softmax(scores, axis=-1)
    rounded = soft_weights.astype(jnp.bfloat16)
    return jnp.einsum('bhqk,bkhc->bqhc', rounded.astype(jnp.float32), valueset.astype(jnp.float32)).astype(jnp.bfloat16)

def attend_backward(queries, keyset, valueset, grad_out):
    factor = HEAD_DIM ** (-0.5)
    scores = jnp.einsum('bqhc,bkhc->bhqk', queries.astype(jnp.float32), keyset.astype(jnp.float32)) * factor
    soft_weights = jax.nn.softmax(scores, axis=-1)
    rounded = soft_weights.astype(jnp.bfloat16).astype(jnp.float32)
    grad_float = grad_out.astype(jnp.float32)
    grad_value = jnp.einsum('bhqk,bqhc->bkhc', rounded, grad_float).astype(jnp.bfloat16)
    grad_probs = jnp.einsum('bqhc,bkhc->bhqk', grad_float, valueset.astype(jnp.float32))
    delta_sum = lax.optimization_barrier(jnp.sum(grad_probs * soft_weights, axis=-1, keepdims=True))
    grad_scores = (soft_weights * (grad_probs - delta_sum) * factor).astype(jnp.bfloat16).astype(jnp.float32)
    grad_query = jnp.einsum('bhqk,bkhc->bqhc', grad_scores, keyset.astype(jnp.float32)).astype(jnp.bfloat16)
    grad_key = jnp.einsum('bhqk,bqhc->bkhc', grad_scores, queries.astype(jnp.float32)).astype(jnp.bfloat16)
    return jnp.stack([grad_query, grad_key, grad_value], axis=2)

def project_qkv(inputs, weights, block_index):
    pieces = [jnp.dot(inputs, weights[:, block_index, slot_index, :], preferred_element_type=jnp.float32).astype(jnp.bfloat16) for slot_index in range(3)]
    return jnp.stack(pieces, axis=1)

def frame_forward(qkv_rows):
    shaped = qkv_rows.reshape(FRAMES, 1, POSITIONS, 3, HEADS, HEAD_DIM)

    def one_frame(block):
        return attend_forward(block[:, :, 0], block[:, :, 1], block[:, :, 2])
    return lax.map(one_frame, shaped).reshape(TOKENS, D)

def frame_backward(qkv_rows, grad_rows):
    shaped = qkv_rows.reshape(FRAMES, 1, POSITIONS, 3, HEADS, HEAD_DIM)
    grad_shaped = grad_rows.reshape(FRAMES, 1, POSITIONS, HEADS, HEAD_DIM)

    def one_frame(blocks):
        block, grad_block = blocks
        return attend_backward(block[:, :, 0], block[:, :, 1], block[:, :, 2], grad_block)
    return lax.map(one_frame, (shaped, grad_shaped)).reshape(TOKENS, 3, D)

def position_split(qkv_rows):
    return qkv_rows.reshape(FRAMES, POSITIONS, 3, HEADS, HEAD_DIM).transpose(1, 0, 2, 3, 4)

def position_forward(qkv_rows):
    split_qkv = position_split(qkv_rows)
    result = attend_forward(split_qkv[:, :, 0], split_qkv[:, :, 1], split_qkv[:, :, 2])
    return result.transpose(1, 0, 2, 3).reshape(TOKENS, D)

def position_backward(qkv_rows, grad_rows):
    split_qkv = position_split(qkv_rows)
    grad_split = grad_rows.reshape(FRAMES, POSITIONS, HEADS, HEAD_DIM).transpose(1, 0, 2, 3)
    result = attend_backward(split_qkv[:, :, 0], split_qkv[:, :, 1], split_qkv[:, :, 2], grad_split)
    return result.transpose(1, 0, 2, 3, 4).reshape(TOKENS, 3, D)

def block_grad(inputs, dqkv, grad_rows, attn_rows):
    pieces = [jnp.dot(inputs.T, dqkv[:, slot_index, :], preferred_element_type=jnp.float32) for slot_index in range(3)]
    pieces.append(jnp.dot(grad_rows.T, attn_rows, preferred_element_type=jnp.float32))
    return jnp.stack(pieces, axis=1)

def clip_forward(clean_latent, clip_noise, step_value, weights):
    clean_rows = clean_latent.astype(jnp.float32)
    target = clip_noise.astype(jnp.float32)
    angle_value = (step_value.astype(jnp.float32) / 1000.0 + 0.008) / 1.008 * (math.pi / 2)
    plan = jnp.cos(angle_value) ** 2
    start_state = jnp.sqrt(plan) * clean_rows + jnp.sqrt(1.0 - plan) * target
    normed_one, inv_one = layer_norm(start_state)
    input_one = normed_one.astype(jnp.bfloat16)
    qkv_one = project_qkv(input_one, weights, 0)
    attn_one = frame_forward(qkv_one)
    state_one = start_state + jnp.dot(attn_one, weights[:, 0, 3, :].T, preferred_element_type=jnp.float32)
    normed_two, inv_two = layer_norm(state_one)
    input_two = normed_two.astype(jnp.bfloat16)
    qkv_two = project_qkv(input_two, weights, 1)
    attn_two = position_forward(qkv_two)
    prediction = state_one + jnp.dot(attn_two, weights[:, 1, 3, :].T, preferred_element_type=jnp.float32)
    diff_rows = prediction - target
    saved = (input_one, qkv_one, attn_one, normed_two, inv_two, input_two, qkv_two, attn_two, diff_rows)
    return (jnp.mean(diff_rows * diff_rows), saved)

def clip_backward(saved, coefficient, weights):
    input_one, qkv_one, attn_one, normed_two, inv_two, input_two, qkv_two, attn_two, diff_rows = saved
    grad_pred = coefficient * 2.0 * diff_rows / D
    grad_two = grad_pred.astype(jnp.bfloat16)
    dout_two = jnp.dot(grad_two, weights[:, 1, 3, :], preferred_element_type=jnp.float32).astype(jnp.bfloat16)
    dqkv_two = position_backward(qkv_two, dout_two)
    dnorm_two = jnp.zeros((TOKENS, D), jnp.float32)
    for slot_index in range(3):
        dnorm_two = dnorm_two + jnp.dot(dqkv_two[:, slot_index, :], weights[:, 1, slot_index, :].T, preferred_element_type=jnp.float32)
    dstate = grad_pred + norm_backward(dnorm_two, normed_two, inv_two)
    grad_one = dstate.astype(jnp.bfloat16)
    dout_one = jnp.dot(grad_one, weights[:, 0, 3, :], preferred_element_type=jnp.float32).astype(jnp.bfloat16)
    dqkv_one = frame_backward(qkv_one, dout_one)
    return jnp.stack([block_grad(input_one, dqkv_one, grad_one, attn_one), block_grad(input_two, dqkv_two, grad_two, attn_two)], axis=1)

def reference(latents, noise, timesteps, ref_losses, weights):
    grad_total = jnp.zeros((D, 2, 4, D), jnp.float32)
    loss_total = jnp.zeros((), jnp.float32)
    for pair_index in range(BATCH):
        error_pair = []
        saved_pair = []
        for clip_index in range(2):
            error_value, saved = clip_forward(latents[clip_index, pair_index], noise[clip_index, pair_index], timesteps[clip_index, pair_index], weights)
            error_pair.append(error_value)
            saved_pair.append(saved)
        margin = error_pair[0] - ref_losses[0, pair_index] - (error_pair[1] - ref_losses[1, pair_index])
        loss_total = loss_total + jax.nn.softplus(beta_dpo * margin)
        for clip_index in range(2):
            signed = 1.0 - 2.0 * clip_index
            coefficient = TOKENS * beta_dpo * jax.nn.sigmoid(beta_dpo * margin) * signed / BATCH
            grad_total = grad_total + clip_backward(saved_pair[clip_index], coefficient, weights)
    return (loss_total / BATCH, grad_total)
```

```python
import functools
import math

import jax
import jax.numpy as jnp
from jax import lax
from jax.experimental import pallas as pl
from jax.experimental.pallas import tpu as pltpu
from jax.sharding import PartitionSpec as P

HEAD_DIM = 72
LANES = 384
NY = 4
MESH = pl.DeviceIdType.MESH
BF = jnp.bfloat16
F32 = jnp.float32

beta_dpo = 0.5
norm_eps = 1e-06


def dot(a, b):
    return jnp.dot(a, b, preferred_element_type=F32)


def dot_nt(a, b):
    return lax.dot_general(a, b, (((1,), (1,)), ((), ())), preferred_element_type=F32)


def dot_tn(a, b):
    return lax.dot_general(a, b, (((0,), (0,)), ((), ())), preferred_element_type=F32)


def iota(shape, axis):
    return lax.broadcasted_iota(jnp.int32, shape, axis)


def head_mask(head, dtype):
    lane = iota((1, LANES), 1)
    return ((lane >= head * HEAD_DIM) & (lane < (head + 1) * HEAD_DIM)).astype(dtype)


def attend_forward(heads, qkv_ref, probs_ref, out_ref, mask):
    queries = qkv_ref[:, :LANES]
    keys = qkv_ref[:, LANES : 2 * LANES]
    values = qkv_ref[:, 2 * LANES :]
    total = None
    for head in range(heads):
        scores = dot_nt(queries * head_mask(head, BF), keys) * (HEAD_DIM**-0.5)
        if mask is not None:
            scores = jnp.where(mask, scores, -1e30)
        scores = jnp.exp(scores - jnp.max(scores, axis=1, keepdims=True))
        probs = scores * (1.0 / jnp.sum(scores, axis=1, keepdims=True))
        probs_ref[head] = probs
        part = dot(probs.astype(BF), values) * head_mask(head, F32)
        total = part if total is None else total + part
    out_ref[...] = total.astype(BF)


def attend_backward(heads, qkv_ref, probs_ref, grad_ref, dqkv_ref):
    queries = qkv_ref[:, :LANES]
    keys = qkv_ref[:, LANES : 2 * LANES]
    values = qkv_ref[:, 2 * LANES :]
    grad = grad_ref[...]
    sums = [None, None, None]
    for head in range(heads):
        probs = probs_ref[head]
        dprobs = dot_nt(grad * head_mask(head, BF), values)
        delta = jnp.sum(dprobs * probs, axis=1, keepdims=True)
        dscores = (probs * (dprobs - delta) * (HEAD_DIM**-0.5)).astype(BF)
        parts = (dot(dscores, keys), dot_tn(dscores, queries), dot_tn(probs.astype(BF), grad))
        for slot in range(3):
            part = parts[slot] * head_mask(head, F32)
            sums[slot] = part if sums[slot] is None else sums[slot] + part
    for slot in range(3):
        dqkv_ref[:, slot * LANES : (slot + 1) * LANES] = sums[slot].astype(BF)


def compact(dqkv_ref):
    dq = dqkv_ref[:, :LANES].astype(F32)
    dk = pltpu.roll(dqkv_ref[:, LANES : 2 * LANES].astype(F32), 32, 1)
    dv = pltpu.roll(dqkv_ref[:, 2 * LANES :].astype(F32), 64, 1)
    return jnp.concatenate(
        [
            dq[:, :256],
            dq[:, 256:] + dk[:, :128],
            dk[:, 128:256],
            dk[:, 256:] + dv[:, :128],
            dv[:, 128:],
        ],
        axis=1,
    ).astype(BF)


def weight_grads(input_ref, compact_ref, grad_ref, attn_ref, out_ref, half_rows):
    attn = pltpu.roll(attn_ref[...].astype(F32), 96, 1).astype(BF)
    dqkv = compact_ref[...]
    step = 128
    for start in range(0, 2 * half_rows, step):
        first = dot_tn(input_ref[:, start : start + step], dqkv)
        second = dot_tn(grad_ref[:, start : start + step], attn)
        rows = jnp.concatenate(
            [first[:, :768], first[:, 768:] + second[:, :128], second[:, 128:]], axis=1
        ).astype(BF)
        done = 0
        while done < step:
            half, at = divmod(start + done, half_rows)
            size = min(step - done, half_rows - at)
            out_ref[half, at : at + size, :] = rows[done : done + size]
            done += size


def pack_matrix(peers, tokens):
    shape = (8 * peers, 3 * peers * tokens)
    row, col = iota(shape, 0), iota(shape, 1)
    peer, inner = row // 8, row % 8
    source = (inner // tokens) * (peers * tokens) + peer * tokens + inner % tokens
    return ((inner < 3 * tokens) & (col == source)).astype(F32).astype(BF)


def unpack_matrix(peers, tokens, third):
    shape = (peers * tokens, 8 * peers)
    token, col = iota(shape, 0), iota(shape, 1)
    source = (token // tokens) * 8 + third * tokens + token % tokens
    return (col == source).astype(F32).astype(BF)


def pack(rows, matrix, peers):
    third = rows.shape[1] // 3
    stacked = jnp.concatenate(
        [rows[:, :third], rows[:, third : 2 * third], rows[:, 2 * third :]], axis=0
    )
    return dot(matrix, stacked).reshape(peers, 8, third)


def unpack(messages, matrices, peers):
    flat = messages.reshape(8 * peers, messages.shape[2]).astype(BF)
    return jnp.concatenate([dot(matrix, flat) for matrix in matrices], axis=1)


def remote(src, dst, send, recv, device):
    return pltpu.make_async_remote_copy(
        src_ref=src,
        dst_ref=dst,
        send_sem=send,
        recv_sem=recv,
        device_id=device,
        device_id_type=MESH,
    )


class RingSum:
    def __init__(self, blocks, low, high, send, recv, me, device, cut):
        self.blocks, self.low, self.high, self.me, self.cut = blocks, low, high, me, cut
        self.right, self.left = (me + 1) % 4, (me + 3) % 4
        opposite = (me + 2) % 4
        rows = blocks.shape[1]
        self.lo, self.hi = pl.ds(0, cut), pl.ds(cut, rows - cut)
        right, left = device(self.right), device(self.left)

        def copy(block, half, dst, index, to):
            return remote(blocks.at[block, half], dst, send.at[index], recv.at[index], to)

        self.far_right = copy(opposite, self.lo, low.at[0], 0, right)
        self.far_left = copy(opposite, self.hi, high.at[0], 1, left)
        self.near_right = copy(self.right, self.hi, high.at[2], 2, right)
        self.near_left = copy(self.left, self.lo, low.at[2], 3, left)
        self.sum_right = copy(self.right, self.lo, low.at[1], 4, right)
        self.sum_left = copy(self.left, self.hi, high.at[1], 5, left)

    def start(self):
        self.far_right.start()
        self.far_left.start()
        self.near_right.start()
        self.near_left.start()

    def middle(self):
        self.far_right.wait_recv()
        own = self.blocks[self.right, self.lo].astype(F32)
        self.blocks[self.right, self.lo] = (own + self.low[0].astype(F32)).astype(BF)
        self.sum_right.start()
        self.far_left.wait_recv()
        own = self.blocks[self.left, self.hi].astype(F32)
        self.blocks[self.left, self.hi] = (own + self.high[0].astype(F32)).astype(BF)
        self.sum_left.start()

    def finish(self):
        self.near_right.wait_recv()
        self.near_left.wait_recv()
        self.sum_right.wait_recv()
        self.sum_left.wait_recv()
        for copy in (self.far_right, self.far_left, self.near_right, self.near_left):
            copy.wait_send()
        self.sum_right.wait_send()
        self.sum_left.wait_send()
        low = self.blocks[self.me, self.lo].astype(F32)
        high = self.blocks[self.me, self.hi].astype(F32)
        low = low + self.low[1].astype(F32) + self.low[2].astype(F32)
        high = high + self.high[1].astype(F32) + self.high[2].astype(F32)
        return jnp.concatenate([low, high], axis=0)


class RingGather:
    def __init__(self, blocks, send, recv, me, device):
        self.right, self.left = (me + 1) % 4, (me + 3) % 4
        half = blocks.shape[1] // 2
        lo, hi = pl.ds(0, half), pl.ds(half, half)
        right, left = device(self.right), device(self.left)

        def copy(block, part, index, to):
            ref = blocks.at[block, part]
            return remote(ref, ref, send.at[index], recv.at[index], to)

        self.first_right = copy(me, lo, 0, right)
        self.first_left = copy(me, hi, 1, left)
        self.next_right = copy(me, hi, 2, right)
        self.next_left = copy(me, lo, 3, left)
        self.pass_right = copy(self.left, lo, 4, right)
        self.pass_left = copy(self.right, hi, 5, left)

    def start(self):
        self.first_right.start()
        self.first_left.start()
        self.next_right.start()
        self.next_left.start()

    def middle(self):
        self.first_right.wait_recv()
        self.pass_right.start()
        self.first_left.wait_recv()
        self.pass_left.start()

    def finish(self):
        for copy in (self.next_right, self.next_left, self.pass_right, self.pass_left):
            copy.wait_recv()
        for copy in (
            self.first_right,
            self.first_left,
            self.next_right,
            self.next_left,
            self.pass_right,
            self.pass_left,
        ):
            copy.wait_send()


class Exchange:
    def __init__(self, out, into, send, recv, me, peers, device):
        self.out, self.into, self.send, self.recv = out, into, send, recv
        self.me, self.peers, self.device = me, peers, device

    def start(self):
        def step(offset, carry):
            peer = (self.me + offset) % self.peers
            remote(
                self.out.at[peer], self.into.at[self.me], self.send, self.recv, self.device(peer)
            ).start()
            return carry

        lax.fori_loop(1, self.peers, step, 0)
        self.into[self.me] = self.out[self.me]

    def finish(self):
        every = pl.ds(0, self.peers - 1)
        remote(
            self.out.at[every],
            self.into.at[every],
            self.send,
            self.recv,
            self.device((self.me + 1) % self.peers),
        ).wait()


def kernel(
    peers,
    heads,
    scale_ref,
    latent_ref,
    noise_ref,
    weights_hbm,
    grads_out,
    errors_out,
    weights_ref,
    weights_sem,
    input_one,
    qkv_one,
    qkv_two,
    probs_one,
    probs_two,
    attn_one,
    attn_two,
    dout_ref,
    dqkv_ref,
    compact_ref,
    start_pos,
    noise_pos,
    state_ref,
    norm_ref,
    grad_ref,
    sum_blocks,
    sum_low,
    sum_high,
    sum_send,
    sum_recv,
    gather_blocks,
    gather_send,
    gather_recv,
    first_out,
    first_in,
    swap_out,
    swap_in,
    swap_send,
    swap_recv,
    partial_ref,
    pair_in,
    pair_send,
    pair_recv,
    y_blocks,
    y_low,
    y_high,
    y_send,
    y_recv,
    z_out,
    z_in,
    z_send,
    z_recv,
    err_x,
    err_x_send,
    err_x_recv,
    err_pair,
    err_pair_send,
    err_pair_recv,
):
    pair, seq, x = lax.axis_index("pair"), lax.axis_index("seq"), lax.axis_index("tensor")
    planes = peers // NY
    y, z = seq // planes, seq % planes
    rows, width = latent_ref.shape
    quarter = rows // 4
    tokens = quarter // peers
    half_rows = width // 2
    y_rows = half_rows // NY
    out_rows = y_rows // planes
    z_rows = z_out.shape[2]

    def at_x(index):
        return (pair, seq, index)

    def at_y(index):
        return (pair, index * planes + z, x)

    def at_z(index):
        return (pair, y * planes + index, x)

    def at_seq(index):
        return (pair, index, x)

    other = (1 - pair, seq, x)

    loads = [
        pltpu.make_async_copy(weights_hbm.at[block], weights_ref.at[block], weights_sem.at[block])
        for block in range(2)
    ]
    for load in loads:
        load.start()

    barrier = pltpu.get_barrier_semaphore()

    def greet(offset, carry):
        pl.semaphore_signal(
            barrier, inc=1, device_id=at_seq((seq + offset) % peers), device_id_type=MESH
        )
        return carry

    lax.fori_loop(1, peers, greet, 0)
    for offset in range(1, 4):
        pl.semaphore_signal(
            barrier, inc=1, device_id=at_x((x + offset) % 4), device_id_type=MESH
        )
    pl.semaphore_signal(barrier, inc=1, device_id=other, device_id_type=MESH)

    ring_sums = [
        RingSum(
            sum_blocks.at[use],
            sum_low.at[use],
            sum_high.at[use],
            sum_send.at[use],
            sum_recv.at[use],
            x,
            at_x,
            quarter // 2,
        )
        for use in range(3)
    ]
    gathers = [
        RingGather(gather_blocks.at[use], gather_send.at[use], gather_recv.at[use], x, at_x)
        for use in range(3)
    ]
    first = Exchange(first_out, first_in, swap_send.at[0], swap_recv.at[0], seq, peers, at_seq)
    swaps = [
        Exchange(
            swap_out.at[use],
            swap_in.at[use],
            swap_send.at[use + 1],
            swap_recv.at[use + 1],
            seq,
            peers,
            at_seq,
        )
        for use in range(2)
    ]
    y_sums = [
        RingSum(
            y_blocks.at[use],
            y_low.at[use],
            y_high.at[use],
            y_send.at[use],
            y_recv.at[use],
            y,
            at_y,
            y_low.shape[2],
        )
        for use in range(2)
    ]
    z_swaps = [
        Exchange(z_out.at[use], z_in.at[use], z_send.at[use], z_recv.at[use], z, planes, at_z)
        for use in range(2)
    ]
    pairs = [
        remote(
            partial_ref.at[use, 1 - pair],
            pair_in.at[use],
            pair_send.at[use],
            pair_recv.at[use],
            other,
        )
        for use in range(2)
    ]

    packing = pack_matrix(peers, tokens)
    unpacking = [unpack_matrix(peers, tokens, third) for third in range(3)]
    clean_scale, noise_scale = scale_ref[0], scale_ref[1]

    mine = pl.ds(pl.multiple_of(x * quarter, quarter), quarter)
    first_out[...] = jnp.concatenate(
        [
            pack(latent_ref[mine, :], packing, peers),
            pack(noise_ref[mine, :], packing, peers),
        ],
        axis=1,
    ).astype(BF)
    pl.semaphore_wait(barrier, peers + 3)
    first.start()

    state = clean_scale * latent_ref[...].astype(F32) + noise_scale * noise_ref[...].astype(F32)
    center = state - jnp.mean(state, axis=1, keepdims=True)
    inv_std = lax.rsqrt(jnp.mean(center * center, axis=1, keepdims=True) + norm_eps)
    input_one[...] = (center * inv_std).astype(BF)
    loads[0].wait()
    qkv_one[...] = dot(input_one[...], weights_ref[0, :, : 3 * LANES]).astype(BF)
    attend_forward(heads, qkv_one, probs_one, attn_one, None)
    sum_blocks[0] = (
        dot_nt(attn_one[...], weights_ref[0, :, 3 * LANES :]).reshape(4, quarter, width).astype(BF)
    )
    ring_sums[0].start()
    ring_sums[0].middle()
    out_one = ring_sums[0].finish()

    swap_out[0] = pack(out_one.astype(BF), packing, peers).astype(BF)
    swaps[0].start()
    first.finish()
    messages = first_in[...].astype(F32)
    clean = unpack(messages[:, :8], unpacking, peers)
    noise_pos[...] = unpack(messages[:, 8:], unpacking, peers)
    start_pos[...] = clean_scale * clean + noise_scale * noise_pos[...]
    swaps[0].finish()
    state = start_pos[...] + unpack(swap_in[0].astype(F32), unpacking, peers)
    state_ref[...] = state
    center = state - jnp.mean(state, axis=1, keepdims=True)
    inv_two = lax.rsqrt(jnp.mean(center * center, axis=1, keepdims=True) + norm_eps)
    norm_ref[...] = center * inv_two
    gather_blocks[0, x] = norm_ref[...].astype(BF)
    gathers[0].start()
    gathers[0].middle()
    gathers[0].finish()

    input_two = gather_blocks.at[0]
    loads[1].wait()
    row, col = iota((rows, rows), 0), iota((rows, rows), 1)
    same = (row // quarter == col // quarter) & (row % tokens == col % tokens)
    flat = input_two[...].reshape(rows, width)
    qkv_two[...] = dot(flat, weights_ref[1, :, : 3 * LANES]).astype(BF)
    attend_forward(heads, qkv_two, probs_two, attn_two, same)
    sum_blocks[1] = (
        dot_nt(attn_two[...], weights_ref[1, :, 3 * LANES :]).reshape(4, quarter, width).astype(BF)
    )
    ring_sums[1].start()
    ring_sums[1].middle()
    diff = state_ref[...] + ring_sums[1].finish() - noise_pos[...]
    error = jnp.sum(jnp.sum(diff * diff, axis=1, keepdims=True), axis=0, keepdims=True)
    sign = 1.0 - 2.0 * pair.astype(F32)
    grad = diff * (2.0 * sign / width)
    grad_ref[...] = grad
    gather_blocks[1, x] = grad.astype(BF)
    gathers[1].start()
    gathers[1].middle()
    gathers[1].finish()

    flat = gather_blocks[1].reshape(rows, width)
    dout_ref[...] = dot(flat, weights_ref[1, :, 3 * LANES :]).astype(BF)
    attend_backward(heads, qkv_two, probs_two, dout_ref, dqkv_ref)
    sum_blocks[2] = (
        dot_nt(dqkv_ref[...], weights_ref[1, :, : 3 * LANES])
        .reshape(4, quarter, width)
        .astype(BF)
    )
    ring_sums[2].start()
    compact_ref[...] = compact(dqkv_ref)
    ring_sums[2].middle()

    def flat_view(use):
        return lambda start, size: gather_blocks[use, :, :, start : start + size].reshape(
            rows, size
        )

    class View:
        def __init__(self, use):
            self.read = flat_view(use)

        def __getitem__(self, index):
            lanes = index[1]
            return self.read(lanes.start, lanes.stop - lanes.start)

    weight_grads(View(0), compact_ref, View(1), attn_two, partial_ref.at[0], half_rows)
    pairs[0].start()
    dnorm = ring_sums[2].finish()
    normed = norm_ref[...]
    mean_grad = jnp.mean(dnorm, axis=1, keepdims=True)
    mean_prod = jnp.mean(dnorm * normed, axis=1, keepdims=True)
    dstate = grad_ref[...] + inv_two * (dnorm - mean_grad - normed * mean_prod)

    messages = pack(dstate.astype(BF), packing, peers)
    inner = iota(messages.shape, 1)
    error_high = error.astype(BF).astype(F32)
    error_low = error - error_high
    messages = jnp.where(inner == 6, error_high.reshape(1, 1, 1), messages)
    messages = jnp.where(inner == 7, error_low.reshape(1, 1, 1), messages)
    swap_out[1] = messages.astype(BF)
    swaps[1].start()

    def reduce_pair(use):
        pairs[use].wait()
        own = partial_ref[use, pair].astype(F32) + pair_in[use].astype(F32)
        y_blocks[use] = own.astype(BF).reshape(NY, y_rows, width)

    shape = (planes * z_rows, y_rows)
    row, col = iota(shape, 0), iota(shape, 1)
    spread = (row % z_rows < out_rows) & (col == (row // z_rows) * out_rows + row % z_rows)
    spread = spread.astype(F32).astype(BF)

    def start_z(use):
        rows_here = y_sums[use].finish().astype(BF)
        z_out[use] = dot(spread, rows_here).reshape(planes, z_rows, width).astype(BF)
        z_swaps[use].start()

    def finish_z(use):
        z_swaps[use].finish()
        grads_out[1 - use] = jnp.sum(z_in[use].astype(F32), axis=0)

    reduce_pair(0)
    y_sums[0].start()
    swaps[1].finish()
    messages = swap_in[1].astype(F32)
    gather_blocks[2, x] = unpack(messages, unpacking, peers).astype(BF)
    gathers[2].start()
    total = jnp.sum(messages, axis=0)
    err_x[x] = jnp.broadcast_to(total[6:7, :128] + total[7:8, :128], (8, 128))
    err_copies = [
        remote(
            err_x.at[x],
            err_x.at[x],
            err_x_send.at[offset - 1],
            err_x_recv.at[offset - 1],
            at_x((x + offset) % 4),
        )
        for offset in range(1, 4)
    ]
    for copy in err_copies:
        copy.start()
    gathers[2].middle()
    y_sums[0].middle()
    gathers[2].finish()

    flat = gather_blocks[2].reshape(rows, width)
    dout_ref[...] = dot(flat, weights_ref[0, :, 3 * LANES :]).astype(BF)
    start_z(0)
    for copy in err_copies:
        copy.wait()
    err_pair[pair] = jnp.sum(err_x[...], axis=0)
    err_copy = remote(
        err_pair.at[pair], err_pair.at[pair], err_pair_send, err_pair_recv, other
    )
    err_copy.start()
    attend_backward(heads, qkv_one, probs_one, dout_ref, dqkv_ref)
    compact_ref[...] = compact(dqkv_ref)
    weight_grads(input_one, compact_ref, View(2), attn_one, partial_ref.at[1], half_rows)
    pairs[1].start()
    finish_z(0)
    err_copy.wait()
    errors_out[...] = err_pair[...]
    reduce_pair(1)
    y_sums[1].start()
    y_sums[1].middle()
    start_z(1)
    finish_z(1)


def local(latents, noise, timesteps, ref_losses, weights):
    width, columns = weights.shape[0], weights.shape[3]
    rows = latents.shape[2]
    peers = lax.axis_size("seq")
    quarter = rows // 4
    planes = peers // NY
    half_rows = width // 2
    y_rows = half_rows // NY
    y_cut = (y_rows // 32 + 1) * 16
    out_rows = y_rows // planes
    z_rows = -(-out_rows // 8) * 8
    heads = columns // HEAD_DIM
    tokens_total = rows * peers

    angle = (timesteps[0, 0].astype(F32) / 1000.0 + 0.008) / 1.008 * (math.pi / 2)
    plan = jnp.cos(angle) ** 2
    scales = jnp.stack([jnp.sqrt(plan), jnp.sqrt(1.0 - plan)])
    padded = jnp.pad(weights, ((0, 0), (0, 0), (0, 0), (0, LANES - columns)))
    padded = padded.transpose(1, 0, 2, 3).reshape(2, width, 4 * LANES)

    vmem = pltpu.VMEM
    dma = pltpu.SemaphoreType.DMA
    third = width // 3
    grads, errors = pl.pallas_call(
        functools.partial(kernel, peers, heads),
        out_shape=(
            jax.ShapeDtypeStruct((2, z_rows, width), F32),
            jax.ShapeDtypeStruct((2, 8, 128), F32),
        ),
        in_specs=[
            pl.BlockSpec(memory_space=pltpu.SMEM),
            pl.BlockSpec(memory_space=vmem),
            pl.BlockSpec(memory_space=vmem),
            pl.BlockSpec(memory_space=pl.ANY),
        ],
        out_specs=(pl.BlockSpec(memory_space=vmem), pl.BlockSpec(memory_space=vmem)),
        scratch_shapes=[
            vmem((2, width, 4 * LANES), BF),
            dma((2,)),
            vmem((rows, width), BF),
            vmem((rows, 3 * LANES), BF),
            vmem((rows, 3 * LANES), BF),
            vmem((heads, rows, rows), F32),
            vmem((heads, rows, rows), F32),
            vmem((rows, LANES), BF),
            vmem((rows, LANES), BF),
            vmem((rows, LANES), BF),
            vmem((rows, 3 * LANES), BF),
            vmem((rows, 896), BF),
            vmem((quarter, width), F32),
            vmem((quarter, width), F32),
            vmem((quarter, width), F32),
            vmem((quarter, width), F32),
            vmem((quarter, width), F32),
            vmem((3, 4, quarter, width), BF),
            vmem((3, 3, quarter // 2, width), BF),
            vmem((3, 3, quarter // 2, width), BF),
            dma((3, 6)),
            dma((3, 6)),
            vmem((3, 4, quarter, width), BF),
            dma((3, 6)),
            dma((3, 6)),
            vmem((peers, 16, third), BF),
            vmem((peers, 16, third), BF),
            vmem((2, peers, 8, third), BF),
            vmem((2, peers, 8, third), BF),
            dma((3,)),
            dma((3,)),
            vmem((2, 2, half_rows, width), BF),
            vmem((2, half_rows, width), BF),
            dma((2,)),
            dma((2,)),
            vmem((2, NY, y_rows, width), BF),
            vmem((2, 3, y_cut, width), BF),
            vmem((2, 3, y_rows - y_cut, width), BF),
            dma((2, 6)),
            dma((2, 6)),
            vmem((2, planes, z_rows, width), BF),
            vmem((2, planes, z_rows, width), BF),
            dma((2,)),
            dma((2,)),
            vmem((4, 8, 128), F32),
            dma((3,)),
            dma((3,)),
            vmem((2, 8, 128), F32),
            dma,
            dma,
        ],
        compiler_params=pltpu.CompilerParams(
            collective_id=0, has_side_effects=True, vmem_limit_bytes=60 * 2**20
        ),
    )(scales, latents[0, 0], noise[0, 0], padded)

    errors = errors[:, 0, 0] / (tokens_total * width)
    margin = errors[0] - ref_losses[0, 0] - (errors[1] - ref_losses[1, 0])
    dpo_loss = jax.nn.softplus(beta_dpo * margin)
    coefficient = tokens_total * beta_dpo * jax.nn.sigmoid(beta_dpo * margin)
    grads = grads[:, :out_rows].reshape(2, out_rows, 4, columns).transpose(1, 0, 2, 3)
    return (dpo_loss, grads * coefficient)


def solution(mesh):
    in_specs = (
        P("pair", None, "seq", None),
        P("pair", None, "seq", None),
        P("pair", None),
        P(),
        P(None, None, None, "tensor"),
    )
    out_specs = (P(), P(("pair", "seq"), None, None, "tensor"))
    return jax.shard_map(local, mesh=mesh, in_specs=in_specs, out_specs=out_specs, check_vma=False)
```

```python
import functools
import math

import jax
import jax.numpy as jnp
from jax import lax
from jax.experimental import pallas as pl
from jax.experimental.pallas import tpu as pltpu
from jax.sharding import PartitionSpec as P

HEAD_DIM = 72
LANES = 384
NY = 4
MESH = pl.DeviceIdType.MESH
BF = jnp.bfloat16
F32 = jnp.float32

beta_dpo = 0.5
norm_eps = 1e-06


def dot(a, b):
    return jnp.dot(a, b, preferred_element_type=F32)


def dot_nt(a, b):
    return lax.dot_general(a, b, (((1,), (1,)), ((), ())), preferred_element_type=F32)


def dot_tn(a, b):
    return lax.dot_general(a, b, (((0,), (0,)), ((), ())), preferred_element_type=F32)


def iota(shape, axis):
    return lax.broadcasted_iota(jnp.int32, shape, axis)


def head_mask(head, dtype):
    lane = iota((1, LANES), 1)
    return ((lane >= head * HEAD_DIM) & (lane < (head + 1) * HEAD_DIM)).astype(dtype)


def attend_forward(heads, qkv_ref, probs_ref, out_ref, mask):
    queries = qkv_ref[:, :LANES]
    keys = qkv_ref[:, LANES : 2 * LANES]
    values = qkv_ref[:, 2 * LANES :]
    total = None
    for head in range(heads):
        scores = dot_nt(queries * head_mask(head, BF), keys) * (HEAD_DIM**-0.5)
        if mask is not None:
            scores = jnp.where(mask, scores, -1e30)
        scores = jnp.exp(scores - jnp.max(scores, axis=1, keepdims=True))
        probs = scores * (1.0 / jnp.sum(scores, axis=1, keepdims=True))
        probs_ref[head] = probs
        part = dot(probs.astype(BF), values) * head_mask(head, F32)
        total = part if total is None else total + part
    out_ref[...] = total.astype(BF)


def attend_backward(heads, qkv_ref, probs_ref, grad_ref, dqkv_ref):
    queries = qkv_ref[:, :LANES]
    keys = qkv_ref[:, LANES : 2 * LANES]
    values = qkv_ref[:, 2 * LANES :]
    grad = grad_ref[...]
    sums = [None, None, None]
    for head in range(heads):
        probs = probs_ref[head]
        dprobs = dot_nt(grad * head_mask(head, BF), values)
        delta = jnp.sum(dprobs * probs, axis=1, keepdims=True)
        dscores = (probs * (dprobs - delta) * (HEAD_DIM**-0.5)).astype(BF)
        parts = (dot(dscores, keys), dot_tn(dscores, queries), dot_tn(probs.astype(BF), grad))
        for slot in range(3):
            part = parts[slot] * head_mask(head, F32)
            sums[slot] = part if sums[slot] is None else sums[slot] + part
    for slot in range(3):
        dqkv_ref[:, slot * LANES : (slot + 1) * LANES] = sums[slot].astype(BF)


def compact(dqkv_ref):
    dq = dqkv_ref[:, :LANES].astype(F32)
    dk = pltpu.roll(dqkv_ref[:, LANES : 2 * LANES].astype(F32), 32, 1)
    dv = pltpu.roll(dqkv_ref[:, 2 * LANES :].astype(F32), 64, 1)
    return jnp.concatenate(
        [
            dq[:, :256],
            dq[:, 256:] + dk[:, :128],
            dk[:, 128:256],
            dk[:, 256:] + dv[:, :128],
            dv[:, 128:],
        ],
        axis=1,
    ).astype(BF)


def weight_grads(input_ref, compact_ref, grad_ref, attn_ref, out_ref, half_rows):
    attn = pltpu.roll(attn_ref[...].astype(F32), 96, 1).astype(BF)
    dqkv = compact_ref[...]
    step = 128
    for start in range(0, 2 * half_rows, step):
        first = dot_tn(input_ref[:, start : start + step], dqkv)
        second = dot_tn(grad_ref[:, start : start + step], attn)
        rows = jnp.concatenate(
            [first[:, :768], first[:, 768:] + second[:, :128], second[:, 128:]], axis=1
        ).astype(BF)
        done = 0
        while done < step:
            half, at = divmod(start + done, half_rows)
            size = min(step - done, half_rows - at)
            out_ref[half, at : at + size, :] = rows[done : done + size]
            done += size


def pack_matrix(peers, tokens):
    shape = (8 * peers, 3 * peers * tokens)
    row, col = iota(shape, 0), iota(shape, 1)
    peer, inner = row // 8, row % 8
    source = (inner // tokens) * (peers * tokens) + peer * tokens + inner % tokens
    return ((inner < 3 * tokens) & (col == source)).astype(F32).astype(BF)


def unpack_matrix(peers, tokens, third):
    shape = (peers * tokens, 8 * peers)
    token, col = iota(shape, 0), iota(shape, 1)
    source = (token // tokens) * 8 + third * tokens + token % tokens
    return (col == source).astype(F32).astype(BF)


def pack(rows, matrix, peers):
    third = rows.shape[1] // 3
    stacked = jnp.concatenate(
        [rows[:, :third], rows[:, third : 2 * third], rows[:, 2 * third :]], axis=0
    )
    return dot(matrix, stacked).reshape(peers, 8, third)


def unpack(messages, matrices, peers):
    flat = messages.reshape(8 * peers, messages.shape[2]).astype(BF)
    return jnp.concatenate([dot(matrix, flat) for matrix in matrices], axis=1)


def remote(src, dst, send, recv, device):
    return pltpu.make_async_remote_copy(
        src_ref=src,
        dst_ref=dst,
        send_sem=send,
        recv_sem=recv,
        device_id=device,
        device_id_type=MESH,
    )


class RingSum:
    def __init__(self, blocks, low, high, send, recv, me, device, cut):
        self.blocks, self.low, self.high, self.me, self.cut = blocks, low, high, me, cut
        self.right, self.left = (me + 1) % 4, (me + 3) % 4
        opposite = (me + 2) % 4
        rows = blocks.shape[1]
        self.lo, self.hi = pl.ds(0, cut), pl.ds(cut, rows - cut)
        right, left = device(self.right), device(self.left)

        def copy(block, half, dst, index, to):
            return remote(blocks.at[block, half], dst, send.at[index], recv.at[index], to)

        self.far_right = copy(opposite, self.lo, low.at[0], 0, right)
        self.far_left = copy(opposite, self.hi, high.at[0], 1, left)
        self.near_right = copy(self.right, self.hi, high.at[2], 2, right)
        self.near_left = copy(self.left, self.lo, low.at[2], 3, left)
        self.sum_right = copy(self.right, self.lo, low.at[1], 4, right)
        self.sum_left = copy(self.left, self.hi, high.at[1], 5, left)

    def start(self):
        self.far_right.start()
        self.far_left.start()
        self.near_right.start()
        self.near_left.start()

    def middle(self):
        self.far_right.wait_recv()
        own = self.blocks[self.right, self.lo].astype(F32)
        self.blocks[self.right, self.lo] = (own + self.low[0].astype(F32)).astype(BF)
        self.sum_right.start()
        self.far_left.wait_recv()
        own = self.blocks[self.left, self.hi].astype(F32)
        self.blocks[self.left, self.hi] = (own + self.high[0].astype(F32)).astype(BF)
        self.sum_left.start()

    def finish(self):
        self.near_right.wait_recv()
        self.near_left.wait_recv()
        self.sum_right.wait_recv()
        self.sum_left.wait_recv()
        for copy in (self.far_right, self.far_left, self.near_right, self.near_left):
            copy.wait_send()
        self.sum_right.wait_send()
        self.sum_left.wait_send()
        low = self.blocks[self.me, self.lo].astype(F32)
        high = self.blocks[self.me, self.hi].astype(F32)
        low = low + self.low[1].astype(F32) + self.low[2].astype(F32)
        high = high + self.high[1].astype(F32) + self.high[2].astype(F32)
        return jnp.concatenate([low, high], axis=0)


class RingGather:
    def __init__(self, blocks, send, recv, me, device):
        self.right, self.left = (me + 1) % 4, (me + 3) % 4
        half = blocks.shape[1] // 2
        lo, hi = pl.ds(0, half), pl.ds(half, half)
        right, left = device(self.right), device(self.left)

        def copy(block, part, index, to):
            ref = blocks.at[block, part]
            return remote(ref, ref, send.at[index], recv.at[index], to)

        self.first_right = copy(me, lo, 0, right)
        self.first_left = copy(me, hi, 1, left)
        self.next_right = copy(me, hi, 2, right)
        self.next_left = copy(me, lo, 3, left)
        self.pass_right = copy(self.left, lo, 4, right)
        self.pass_left = copy(self.right, hi, 5, left)

    def start(self):
        self.first_right.start()
        self.first_left.start()
        self.next_right.start()
        self.next_left.start()

    def middle(self):
        self.first_right.wait_recv()
        self.pass_right.start()
        self.first_left.wait_recv()
        self.pass_left.start()

    def finish(self):
        for copy in (self.next_right, self.next_left, self.pass_right, self.pass_left):
            copy.wait_recv()
        for copy in (
            self.first_right,
            self.first_left,
            self.next_right,
            self.next_left,
            self.pass_right,
            self.pass_left,
        ):
            copy.wait_send()


class Exchange:
    def __init__(self, out, into, send, recv, me, peers, device):
        self.out, self.into, self.send, self.recv = out, into, send, recv
        self.me, self.peers, self.device = me, peers, device

    def start(self):
        def step(offset, carry):
            peer = (self.me + offset) % self.peers
            remote(
                self.out.at[peer], self.into.at[self.me], self.send, self.recv, self.device(peer)
            ).start()
            return carry

        lax.fori_loop(1, self.peers, step, 0)
        self.into[self.me] = self.out[self.me]

    def finish(self):
        every = pl.ds(0, self.peers - 1)
        remote(
            self.out.at[every],
            self.into.at[every],
            self.send,
            self.recv,
            self.device((self.me + 1) % self.peers),
        ).wait()


def kernel(
    peers,
    heads,
    scale_ref,
    ref_losses,
    latent_ref,
    noise_ref,
    weights_hbm,
    grads_out,
    loss_out,
    weights_ref,
    weights_sem,
    input_one,
    qkv_one,
    qkv_two,
    probs_one,
    probs_two,
    attn_one,
    attn_two,
    dout_ref,
    dqkv_ref,
    compact_ref,
    start_pos,
    noise_pos,
    state_ref,
    norm_ref,
    grad_ref,
    sum_blocks,
    sum_low,
    sum_high,
    sum_send,
    sum_recv,
    gather_blocks,
    gather_send,
    gather_recv,
    first_out,
    first_in,
    swap_out,
    swap_in,
    swap_send,
    swap_recv,
    partial_ref,
    pair_in,
    pair_send,
    pair_recv,
    y_blocks,
    y_low,
    y_high,
    y_send,
    y_recv,
    z_out,
    z_in,
    z_send,
    z_recv,
    err_x,
    err_x_send,
    err_x_recv,
    err_pair,
    err_pair_send,
    err_pair_recv,
):
    pair, seq, x = lax.axis_index("pair"), lax.axis_index("seq"), lax.axis_index("tensor")
    planes = peers // NY
    y, z = seq // planes, seq % planes
    rows, width = latent_ref.shape
    quarter = rows // 4
    tokens = quarter // peers
    half_rows = width // 2
    y_rows = half_rows // NY
    out_rows = y_rows // planes
    z_rows = z_out.shape[2]

    def at_x(index):
        return (pair, seq, index)

    def at_y(index):
        return (pair, index * planes + z, x)

    def at_z(index):
        return (pair, y * planes + index, x)

    def at_seq(index):
        return (pair, index, x)

    other = (1 - pair, seq, x)

    columns = weights_hbm.shape[2]
    loads = [
        [
            pltpu.make_async_copy(
                weights_hbm.at[block, slot],
                weights_ref.at[block, pl.ds(slot * LANES, columns)],
                weights_sem.at[block, slot],
            )
            for slot in range(4)
        ]
        for block in range(2)
    ]
    for load in loads[0] + loads[1]:
        load.start()
    for slot in range(4):
        for block in range(2):
            weights_ref[block, slot * LANES + columns : (slot + 1) * LANES, :] = jnp.zeros(
                (LANES - columns, width), BF
            )

    barrier = pltpu.get_barrier_semaphore()

    def greet(offset, carry):
        pl.semaphore_signal(
            barrier, inc=1, device_id=at_seq((seq + offset) % peers), device_id_type=MESH
        )
        return carry

    lax.fori_loop(1, peers, greet, 0)
    for offset in range(1, 4):
        pl.semaphore_signal(
            barrier, inc=1, device_id=at_x((x + offset) % 4), device_id_type=MESH
        )
    pl.semaphore_signal(barrier, inc=1, device_id=other, device_id_type=MESH)

    ring_sums = [
        RingSum(
            sum_blocks.at[use],
            sum_low.at[use],
            sum_high.at[use],
            sum_send.at[use],
            sum_recv.at[use],
            x,
            at_x,
            quarter // 2,
        )
        for use in range(3)
    ]
    gathers = [
        RingGather(gather_blocks.at[use], gather_send.at[use], gather_recv.at[use], x, at_x)
        for use in range(3)
    ]
    first = Exchange(first_out, first_in, swap_send.at[0], swap_recv.at[0], seq, peers, at_seq)
    swaps = [
        Exchange(
            swap_out.at[use],
            swap_in.at[use],
            swap_send.at[use + 1],
            swap_recv.at[use + 1],
            seq,
            peers,
            at_seq,
        )
        for use in range(2)
    ]
    y_sums = [
        RingSum(
            y_blocks.at[use],
            y_low.at[use],
            y_high.at[use],
            y_send.at[use],
            y_recv.at[use],
            y,
            at_y,
            y_low.shape[2],
        )
        for use in range(2)
    ]
    z_swaps = [
        Exchange(z_out.at[use], z_in.at[use], z_send.at[use], z_recv.at[use], z, planes, at_z)
        for use in range(2)
    ]
    pairs = [
        remote(
            partial_ref.at[use, 1 - pair],
            pair_in.at[use],
            pair_send.at[use],
            pair_recv.at[use],
            other,
        )
        for use in range(2)
    ]

    packing = pack_matrix(peers, tokens)
    unpacking = [unpack_matrix(peers, tokens, third) for third in range(3)]
    clean_scale, noise_scale = scale_ref[0], scale_ref[1]

    mine = pl.ds(pl.multiple_of(x * quarter, quarter), quarter)
    first_out[...] = jnp.concatenate(
        [
            pack(latent_ref[mine, :], packing, peers),
            pack(noise_ref[mine, :], packing, peers),
        ],
        axis=1,
    ).astype(BF)
    pl.semaphore_wait(barrier, peers + 3)
    first.start()

    state = clean_scale * latent_ref[...].astype(F32) + noise_scale * noise_ref[...].astype(F32)
    center = state - jnp.mean(state, axis=1, keepdims=True)
    inv_std = lax.rsqrt(jnp.mean(center * center, axis=1, keepdims=True) + norm_eps)
    input_one[...] = (center * inv_std).astype(BF)
    for load in loads[0]:
        load.wait()
    qkv_one[...] = dot_nt(input_one[...], weights_ref[0, : 3 * LANES]).astype(BF)
    attend_forward(heads, qkv_one, probs_one, attn_one, None)
    sum_blocks[0] = (
        dot(attn_one[...], weights_ref[0, 3 * LANES :]).reshape(4, quarter, width).astype(BF)
    )
    ring_sums[0].start()
    ring_sums[0].middle()
    out_one = ring_sums[0].finish()

    swap_out[0] = pack(out_one.astype(BF), packing, peers).astype(BF)
    swaps[0].start()
    first.finish()
    messages = first_in[...].astype(F32)
    clean = unpack(messages[:, :8], unpacking, peers)
    noise_pos[...] = unpack(messages[:, 8:], unpacking, peers)
    start_pos[...] = clean_scale * clean + noise_scale * noise_pos[...]
    swaps[0].finish()
    state = start_pos[...] + unpack(swap_in[0].astype(F32), unpacking, peers)
    state_ref[...] = state
    center = state - jnp.mean(state, axis=1, keepdims=True)
    inv_two = lax.rsqrt(jnp.mean(center * center, axis=1, keepdims=True) + norm_eps)
    norm_ref[...] = center * inv_two
    gather_blocks[0, x] = norm_ref[...].astype(BF)
    gathers[0].start()
    gathers[0].middle()
    gathers[0].finish()

    input_two = gather_blocks.at[0]
    for load in loads[1]:
        load.wait()
    row, col = iota((rows, rows), 0), iota((rows, rows), 1)
    same = (row // quarter == col // quarter) & (row % tokens == col % tokens)
    flat = input_two[...].reshape(rows, width)
    qkv_two[...] = dot_nt(flat, weights_ref[1, : 3 * LANES]).astype(BF)
    attend_forward(heads, qkv_two, probs_two, attn_two, same)
    sum_blocks[1] = (
        dot(attn_two[...], weights_ref[1, 3 * LANES :]).reshape(4, quarter, width).astype(BF)
    )
    ring_sums[1].start()
    ring_sums[1].middle()
    diff = state_ref[...] + ring_sums[1].finish() - noise_pos[...]
    error = jnp.sum(jnp.sum(diff * diff, axis=1, keepdims=True), axis=0, keepdims=True)
    sign = 1.0 - 2.0 * pair.astype(F32)
    grad = diff * (2.0 * sign / width)
    grad_ref[...] = grad
    gather_blocks[1, x] = grad.astype(BF)
    gathers[1].start()
    gathers[1].middle()
    gathers[1].finish()

    flat = gather_blocks[1].reshape(rows, width)
    dout_ref[...] = dot_nt(flat, weights_ref[1, 3 * LANES :]).astype(BF)
    attend_backward(heads, qkv_two, probs_two, dout_ref, dqkv_ref)
    sum_blocks[2] = (
        dot(dqkv_ref[...], weights_ref[1, : 3 * LANES])
        .reshape(4, quarter, width)
        .astype(BF)
    )
    ring_sums[2].start()
    compact_ref[...] = compact(dqkv_ref)
    ring_sums[2].middle()

    def flat_view(use):
        return lambda start, size: gather_blocks[use, :, :, start : start + size].reshape(
            rows, size
        )

    class View:
        def __init__(self, use):
            self.read = flat_view(use)

        def __getitem__(self, index):
            lanes = index[1]
            return self.read(lanes.start, lanes.stop - lanes.start)

    weight_grads(View(0), compact_ref, View(1), attn_two, partial_ref.at[0], half_rows)
    pairs[0].start()
    dnorm = ring_sums[2].finish()
    normed = norm_ref[...]
    mean_grad = jnp.mean(dnorm, axis=1, keepdims=True)
    mean_prod = jnp.mean(dnorm * normed, axis=1, keepdims=True)
    dstate = grad_ref[...] + inv_two * (dnorm - mean_grad - normed * mean_prod)

    messages = pack(dstate.astype(BF), packing, peers)
    inner = iota(messages.shape, 1)
    error_high = error.astype(BF).astype(F32)
    error_low = error - error_high
    messages = jnp.where(inner == 6, error_high.reshape(1, 1, 1), messages)
    messages = jnp.where(inner == 7, error_low.reshape(1, 1, 1), messages)
    swap_out[1] = messages.astype(BF)
    swaps[1].start()

    def reduce_pair(use):
        pairs[use].wait()
        own = partial_ref[use, pair].astype(F32) + pair_in[use].astype(F32)
        y_blocks[use] = own.astype(BF).reshape(NY, y_rows, width)

    shape = (planes * z_rows, y_rows)
    row, col = iota(shape, 0), iota(shape, 1)
    spread = (row % z_rows < out_rows) & (col == (row // z_rows) * out_rows + row % z_rows)
    spread = spread.astype(F32).astype(BF)

    def start_z(use):
        rows_here = y_sums[use].finish().astype(BF)
        z_out[use] = dot(spread, rows_here).reshape(planes, z_rows, width).astype(BF)
        z_swaps[use].start()

    def finish_z(use):
        z_swaps[use].finish()
        return jnp.sum(z_in[use].astype(F32), axis=0)

    reduce_pair(0)
    y_sums[0].start()
    swaps[1].finish()
    messages = swap_in[1].astype(F32)
    gather_blocks[2, x] = unpack(messages, unpacking, peers).astype(BF)
    gathers[2].start()
    total = jnp.sum(messages, axis=0)
    err_x[x] = jnp.broadcast_to(total[6:7, :128] + total[7:8, :128], (8, 128))
    err_copies = [
        remote(
            err_x.at[x],
            err_x.at[x],
            err_x_send.at[offset - 1],
            err_x_recv.at[offset - 1],
            at_x((x + offset) % 4),
        )
        for offset in range(1, 4)
    ]
    for copy in err_copies:
        copy.start()
    gathers[2].middle()
    y_sums[0].middle()
    gathers[2].finish()

    flat = gather_blocks[2].reshape(rows, width)
    dout_ref[...] = dot_nt(flat, weights_ref[0, 3 * LANES :]).astype(BF)
    start_z(0)
    for copy in err_copies:
        copy.wait()
    err_pair[pair] = jnp.sum(err_x[...], axis=0)
    err_copy = remote(
        err_pair.at[pair], err_pair.at[pair], err_pair_send, err_pair_recv, other
    )
    err_copy.start()
    attend_backward(heads, qkv_one, probs_one, dout_ref, dqkv_ref)
    compact_ref[...] = compact(dqkv_ref)
    weight_grads(input_one, compact_ref, View(2), attn_one, partial_ref.at[1], half_rows)
    pairs[1].start()
    second_grads = finish_z(0)
    err_copy.wait()
    margin = (err_pair[0] - err_pair[1]) * (1.0 / (rows * peers * width))
    scaled = beta_dpo * (margin - (ref_losses[0] - ref_losses[1]))
    loss_out[...] = jnp.maximum(scaled, 0.0) + jnp.log1p(jnp.exp(-jnp.abs(scaled)))
    factor = (rows * peers * beta_dpo) * jax.nn.sigmoid(scaled)
    factor = factor[:1, :1]
    reduce_pair(1)
    y_sums[1].start()
    y_sums[1].middle()
    start_z(1)
    grads_out[1] = second_grads * factor
    grads_out[0] = finish_z(1) * factor


def local(latents, noise, timesteps, ref_losses, weights):
    width, columns = weights.shape[0], weights.shape[3]
    rows = latents.shape[2]
    peers = lax.axis_size("seq")
    quarter = rows // 4
    planes = peers // NY
    half_rows = width // 2
    y_rows = half_rows // NY
    y_cut = (y_rows // 32 + 1) * 16
    out_rows = y_rows // planes
    z_rows = -(-out_rows // 8) * 8
    heads = columns // HEAD_DIM

    angle = (timesteps[0, 0].astype(F32) / 1000.0 + 0.008) / 1.008 * (math.pi / 2)
    plan = jnp.cos(angle) ** 2
    scales = jnp.stack([jnp.sqrt(plan), jnp.sqrt(1.0 - plan)])

    vmem = pltpu.VMEM
    dma = pltpu.SemaphoreType.DMA
    third = width // 3
    grads, loss = pl.pallas_call(
        functools.partial(kernel, peers, heads),
        out_shape=(
            jax.ShapeDtypeStruct((2, z_rows, width), F32),
            jax.ShapeDtypeStruct((8, 128), F32),
        ),
        in_specs=[
            pl.BlockSpec(memory_space=pltpu.SMEM),
            pl.BlockSpec(memory_space=pltpu.SMEM),
            pl.BlockSpec(memory_space=vmem),
            pl.BlockSpec(memory_space=vmem),
            pl.BlockSpec(memory_space=pl.ANY),
        ],
        out_specs=(pl.BlockSpec(memory_space=vmem), pl.BlockSpec(memory_space=vmem)),
        scratch_shapes=[
            vmem((2, 4 * LANES, width), BF),
            dma((2, 4)),
            vmem((rows, width), BF),
            vmem((rows, 3 * LANES), BF),
            vmem((rows, 3 * LANES), BF),
            vmem((heads, rows, rows), F32),
            vmem((heads, rows, rows), F32),
            vmem((rows, LANES), BF),
            vmem((rows, LANES), BF),
            vmem((rows, LANES), BF),
            vmem((rows, 3 * LANES), BF),
            vmem((rows, 896), BF),
            vmem((quarter, width), F32),
            vmem((quarter, width), F32),
            vmem((quarter, width), F32),
            vmem((quarter, width), F32),
            vmem((quarter, width), F32),
            vmem((3, 4, quarter, width), BF),
            vmem((3, 3, quarter // 2, width), BF),
            vmem((3, 3, quarter // 2, width), BF),
            dma((3, 6)),
            dma((3, 6)),
            vmem((3, 4, quarter, width), BF),
            dma((3, 6)),
            dma((3, 6)),
            vmem((peers, 16, third), BF),
            vmem((peers, 16, third), BF),
            vmem((2, peers, 8, third), BF),
            vmem((2, peers, 8, third), BF),
            dma((3,)),
            dma((3,)),
            vmem((2, 2, half_rows, width), BF),
            vmem((2, half_rows, width), BF),
            dma((2,)),
            dma((2,)),
            vmem((2, NY, y_rows, width), BF),
            vmem((2, 3, y_cut, width), BF),
            vmem((2, 3, y_rows - y_cut, width), BF),
            dma((2, 6)),
            dma((2, 6)),
            vmem((2, planes, z_rows, width), BF),
            vmem((2, planes, z_rows, width), BF),
            dma((2,)),
            dma((2,)),
            vmem((4, 8, 128), F32),
            dma((3,)),
            dma((3,)),
            vmem((2, 8, 128), F32),
            dma,
            dma,
        ],
        compiler_params=pltpu.CompilerParams(
            collective_id=0, has_side_effects=True, vmem_limit_bytes=60 * 2**20
        ),
    )(scales, ref_losses[:, 0], latents[0, 0], noise[0, 0], weights.transpose(1, 2, 3, 0))

    grads = grads[:, :out_rows].reshape(2, out_rows, 4, columns).transpose(1, 0, 2, 3)
    return (loss[0, 0], grads)


def solution(mesh):
    in_specs = (
        P("pair", None, "seq", None),
        P("pair", None, "seq", None),
        P("pair", None),
        P(),
        P(None, None, None, "tensor"),
    )
    out_specs = (P(), P(("pair", "seq"), None, None, "tensor"))
    return jax.shard_map(local, mesh=mesh, in_specs=in_specs, out_specs=out_specs, check_vma=False)
```

```python
import functools
import math

import jax
import jax.numpy as jnp
from jax import lax
from jax.experimental import pallas as pl
from jax.experimental.pallas import tpu as pltpu
from jax.sharding import PartitionSpec as P

HEAD_DIM = 72
LANES = 384
NY = 4
MESH = pl.DeviceIdType.MESH
BF = jnp.bfloat16
F32 = jnp.float32

beta_dpo = 0.5
norm_eps = 1e-06


def dot(a, b):
    return jnp.dot(a, b, preferred_element_type=F32)


def dot_nt(a, b):
    return lax.dot_general(a, b, (((1,), (1,)), ((), ())), preferred_element_type=F32)


def dot_tn(a, b):
    return lax.dot_general(a, b, (((0,), (0,)), ((), ())), preferred_element_type=F32)


def iota(shape, axis):
    return lax.broadcasted_iota(jnp.int32, shape, axis)


def head_mask(head, dtype):
    lane = iota((1, LANES), 1)
    return ((lane >= head * HEAD_DIM) & (lane < (head + 1) * HEAD_DIM)).astype(dtype)


def attend_forward(heads, qkv_ref, probs_ref, out_ref, mask):
    queries = qkv_ref[:, :LANES]
    keys = qkv_ref[:, LANES : 2 * LANES]
    values = qkv_ref[:, 2 * LANES :]
    total = None
    for head in range(heads):
        scores = dot_nt(queries * head_mask(head, BF), keys) * (HEAD_DIM**-0.5)
        if mask is not None:
            scores = jnp.where(mask, scores, -1e30)
        scores = jnp.exp(scores - jnp.max(scores, axis=1, keepdims=True))
        probs = scores * (1.0 / jnp.sum(scores, axis=1, keepdims=True))
        probs_ref[head] = probs
        part = dot(probs.astype(BF), values) * head_mask(head, F32)
        total = part if total is None else total + part
    out_ref[...] = total.astype(BF)


def attend_backward(heads, qkv_ref, probs_ref, grad_ref, dqkv_ref):
    queries = qkv_ref[:, :LANES]
    keys = qkv_ref[:, LANES : 2 * LANES]
    values = qkv_ref[:, 2 * LANES :]
    grad = grad_ref[...]
    sums = [None, None, None]
    for head in range(heads):
        probs = probs_ref[head]
        dprobs = dot_nt(grad * head_mask(head, BF), values)
        delta = jnp.sum(dprobs * probs, axis=1, keepdims=True)
        dscores = (probs * (dprobs - delta) * (HEAD_DIM**-0.5)).astype(BF)
        parts = (dot(dscores, keys), dot_tn(dscores, queries), dot_tn(probs.astype(BF), grad))
        for slot in range(3):
            part = parts[slot] * head_mask(head, F32)
            sums[slot] = part if sums[slot] is None else sums[slot] + part
    for slot in range(3):
        dqkv_ref[:, slot * LANES : (slot + 1) * LANES] = sums[slot].astype(BF)


def compact(dqkv_ref):
    dq = dqkv_ref[:, :LANES].astype(F32)
    dk = pltpu.roll(dqkv_ref[:, LANES : 2 * LANES].astype(F32), 32, 1)
    dv = pltpu.roll(dqkv_ref[:, 2 * LANES :].astype(F32), 64, 1)
    return jnp.concatenate(
        [
            dq[:, :256],
            dq[:, 256:] + dk[:, :128],
            dk[:, 128:256],
            dk[:, 256:] + dv[:, :128],
            dv[:, 128:],
        ],
        axis=1,
    ).astype(BF)


def weight_grads(input_ref, compact_ref, grad_ref, attn_ref, out_ref, half_rows):
    attn = pltpu.roll(attn_ref[...].astype(F32), 96, 1).astype(BF)
    dqkv = compact_ref[...]
    step = 128
    for start in range(0, 2 * half_rows, step):
        first = dot_tn(input_ref[:, start : start + step], dqkv)
        second = dot_tn(grad_ref[:, start : start + step], attn)
        rows = jnp.concatenate(
            [first[:, :768], first[:, 768:] + second[:, :128], second[:, 128:]], axis=1
        ).astype(BF)
        done = 0
        while done < step:
            half, at = divmod(start + done, half_rows)
            size = min(step - done, half_rows - at)
            out_ref[half, at : at + size, :] = rows[done : done + size]
            done += size


def pack_matrix(peers, tokens):
    shape = (8 * peers, 3 * peers * tokens)
    row, col = iota(shape, 0), iota(shape, 1)
    peer, inner = row // 8, row % 8
    source = (inner // tokens) * (peers * tokens) + peer * tokens + inner % tokens
    return ((inner < 3 * tokens) & (col == source)).astype(F32).astype(BF)


def unpack_matrix(peers, tokens, third):
    shape = (peers * tokens, 8 * peers)
    token, col = iota(shape, 0), iota(shape, 1)
    source = (token // tokens) * 8 + third * tokens + token % tokens
    return (col == source).astype(F32).astype(BF)


def pack(rows, matrix, peers):
    third = rows.shape[1] // 3
    stacked = jnp.concatenate(
        [rows[:, :third], rows[:, third : 2 * third], rows[:, 2 * third :]], axis=0
    )
    return dot(matrix, stacked).reshape(peers, 8, third)


def unpack(messages, matrices, peers):
    flat = messages.reshape(8 * peers, messages.shape[2]).astype(BF)
    return jnp.concatenate([dot(matrix, flat) for matrix in matrices], axis=1)


def remote(src, dst, send, recv, device):
    return pltpu.make_async_remote_copy(
        src_ref=src,
        dst_ref=dst,
        send_sem=send,
        recv_sem=recv,
        device_id=device,
        device_id_type=MESH,
    )


class RingSum:
    def __init__(self, blocks, low, high, send, recv, me, device, cut):
        self.blocks, self.low, self.high, self.me, self.cut = blocks, low, high, me, cut
        self.right, self.left = (me + 1) % 4, (me + 3) % 4
        self.opposite = opposite = (me + 2) % 4
        rows = blocks.shape[1]
        self.lo, self.hi = pl.ds(0, cut), pl.ds(cut, rows - cut)
        right, left = device(self.right), device(self.left)

        def copy(block, half, dst, index, to):
            return remote(blocks.at[block, half], dst, send.at[index], recv.at[index], to)

        self.far_right = copy(opposite, self.lo, low.at[0], 0, right)
        self.far_left = copy(opposite, self.hi, high.at[0], 1, left)
        self.near_right = copy(self.right, self.hi, high.at[2], 2, right)
        self.near_left = copy(self.left, self.lo, low.at[2], 3, left)
        self.sum_right = copy(self.right, self.lo, low.at[1], 4, right)
        self.sum_left = copy(self.left, self.hi, high.at[1], 5, left)

    def start(self, fill=None):
        if fill is not None:
            fill(self.opposite, self.right)
        self.far_right.start()
        self.far_left.start()
        self.near_right.start()
        if fill is not None:
            fill(self.left, self.me)
        self.near_left.start()

    def middle(self):
        self.far_right.wait_recv()
        own = self.blocks[self.right, self.lo].astype(F32)
        self.blocks[self.right, self.lo] = (own + self.low[0].astype(F32)).astype(BF)
        self.sum_right.start()
        self.far_left.wait_recv()
        own = self.blocks[self.left, self.hi].astype(F32)
        self.blocks[self.left, self.hi] = (own + self.high[0].astype(F32)).astype(BF)
        self.sum_left.start()

    def finish(self):
        self.near_right.wait_recv()
        self.near_left.wait_recv()
        self.sum_right.wait_recv()
        self.sum_left.wait_recv()
        for copy in (self.far_right, self.far_left, self.near_right, self.near_left):
            copy.wait_send()
        self.sum_right.wait_send()
        self.sum_left.wait_send()
        low = self.blocks[self.me, self.lo].astype(F32)
        high = self.blocks[self.me, self.hi].astype(F32)
        low = low + self.low[1].astype(F32) + self.low[2].astype(F32)
        high = high + self.high[1].astype(F32) + self.high[2].astype(F32)
        return jnp.concatenate([low, high], axis=0)


class RingGather:
    def __init__(self, blocks, send, recv, me, device):
        self.blocks, self.me = blocks, me
        self.right, self.left = (me + 1) % 4, (me + 3) % 4
        self.opposite = (me + 2) % 4
        half = blocks.shape[1] // 2
        lo, hi = pl.ds(0, half), pl.ds(half, half)
        right, left = device(self.right), device(self.left)

        def copy(block, part, index, to):
            ref = blocks.at[block, part]
            return remote(ref, ref, send.at[index], recv.at[index], to)

        self.first_right = copy(me, lo, 0, right)
        self.first_left = copy(me, hi, 1, left)
        self.next_right = copy(me, hi, 2, right)
        self.next_left = copy(me, lo, 3, left)
        self.pass_right = copy(self.left, lo, 4, right)
        self.pass_left = copy(self.right, hi, 5, left)

    def start(self):
        self.first_right.start()
        self.first_left.start()
        self.next_right.start()
        self.next_left.start()

    def middle(self):
        self.first_right.wait_recv()
        self.pass_right.start()
        self.first_left.wait_recv()
        self.pass_left.start()

    def project(self, weights, out_ref):
        size = self.blocks.shape[1]
        self.next_right.wait_recv()
        self.next_left.wait_recv()
        near = (self.me, self.left, self.right)
        result = dot_nt(jnp.concatenate([self.blocks[block] for block in near], axis=0), weights)
        for place, block in enumerate(near):
            out_ref[pl.ds(pl.multiple_of(block * size, size), size), :] = result[
                place * size : (place + 1) * size
            ].astype(BF)
        self.pass_right.wait_recv()
        self.pass_left.wait_recv()
        out_ref[pl.ds(pl.multiple_of(self.opposite * size, size), size), :] = dot_nt(
            self.blocks[self.opposite], weights
        ).astype(BF)
        for copy in (
            self.first_right,
            self.first_left,
            self.next_right,
            self.next_left,
            self.pass_right,
            self.pass_left,
        ):
            copy.wait_send()


class Exchange:
    def __init__(self, out, into, send, recv, me, peers, device):
        self.out, self.into, self.send, self.recv = out, into, send, recv
        self.me, self.peers, self.device = me, peers, device

    def start(self):
        def step(offset, carry):
            peer = (self.me + offset) % self.peers
            remote(
                self.out.at[peer], self.into.at[self.me], self.send, self.recv, self.device(peer)
            ).start()
            return carry

        lax.fori_loop(1, self.peers, step, 0)
        self.into[self.me] = self.out[self.me]

    def finish(self):
        every = pl.ds(0, self.peers - 1)
        remote(
            self.out.at[every],
            self.into.at[every],
            self.send,
            self.recv,
            self.device((self.me + 1) % self.peers),
        ).wait()


def kernel(
    peers,
    heads,
    scale_ref,
    ref_losses,
    latent_ref,
    noise_ref,
    weights_hbm,
    grads_out,
    loss_out,
    weights_ref,
    weights_sem,
    input_one,
    qkv_one,
    qkv_two,
    probs_one,
    probs_two,
    attn_one,
    attn_two,
    dout_ref,
    dqkv_ref,
    compact_ref,
    start_pos,
    noise_pos,
    state_ref,
    norm_ref,
    grad_ref,
    sum_blocks,
    sum_low,
    sum_high,
    sum_send,
    sum_recv,
    gather_blocks,
    gather_send,
    gather_recv,
    first_out,
    first_in,
    swap_out,
    swap_in,
    swap_send,
    swap_recv,
    partial_ref,
    pair_in,
    pair_send,
    pair_recv,
    y_blocks,
    y_low,
    y_high,
    y_send,
    y_recv,
    z_out,
    z_in,
    z_send,
    z_recv,
    err_x,
    err_x_send,
    err_x_recv,
    err_pair,
    err_pair_send,
    err_pair_recv,
):
    pair, seq, x = lax.axis_index("pair"), lax.axis_index("seq"), lax.axis_index("tensor")
    planes = peers // NY
    y, z = seq // planes, seq % planes
    rows, width = latent_ref.shape
    quarter = rows // 4
    tokens = quarter // peers
    half_rows = width // 2
    y_rows = half_rows // NY
    out_rows = y_rows // planes
    z_rows = z_out.shape[2]

    def at_x(index):
        return (pair, seq, index)

    def at_y(index):
        return (pair, index * planes + z, x)

    def at_z(index):
        return (pair, y * planes + index, x)

    def at_seq(index):
        return (pair, index, x)

    other = (1 - pair, seq, x)

    columns = weights_hbm.shape[2]
    loads = [
        [
            pltpu.make_async_copy(
                weights_hbm.at[block, slot],
                weights_ref.at[block, pl.ds(slot * LANES, columns)],
                weights_sem.at[block, slot],
            )
            for slot in range(4)
        ]
        for block in range(2)
    ]
    for load in loads[0] + loads[1]:
        load.start()
    for slot in range(4):
        for block in range(2):
            weights_ref[block, slot * LANES + columns : (slot + 1) * LANES, :] = jnp.zeros(
                (LANES - columns, width), BF
            )

    barrier = pltpu.get_barrier_semaphore()

    def greet(offset, carry):
        pl.semaphore_signal(
            barrier, inc=1, device_id=at_seq((seq + offset) % peers), device_id_type=MESH
        )
        return carry

    lax.fori_loop(1, peers, greet, 0)
    for offset in range(1, 4):
        pl.semaphore_signal(
            barrier, inc=1, device_id=at_x((x + offset) % 4), device_id_type=MESH
        )
    pl.semaphore_signal(barrier, inc=1, device_id=other, device_id_type=MESH)

    ring_sums = [
        RingSum(
            sum_blocks.at[use],
            sum_low.at[use],
            sum_high.at[use],
            sum_send.at[use],
            sum_recv.at[use],
            x,
            at_x,
            quarter // 2,
        )
        for use in range(3)
    ]
    gathers = [
        RingGather(gather_blocks.at[use], gather_send.at[use], gather_recv.at[use], x, at_x)
        for use in range(3)
    ]
    first = Exchange(first_out, first_in, swap_send.at[0], swap_recv.at[0], seq, peers, at_seq)
    swaps = [
        Exchange(
            swap_out.at[use],
            swap_in.at[use],
            swap_send.at[use + 1],
            swap_recv.at[use + 1],
            seq,
            peers,
            at_seq,
        )
        for use in range(2)
    ]
    y_sums = [
        RingSum(
            y_blocks.at[use],
            y_low.at[use],
            y_high.at[use],
            y_send.at[use],
            y_recv.at[use],
            y,
            at_y,
            y_low.shape[2],
        )
        for use in range(2)
    ]
    z_swaps = [
        Exchange(z_out.at[use], z_in.at[use], z_send.at[use], z_recv.at[use], z, planes, at_z)
        for use in range(2)
    ]
    pairs = [
        remote(
            partial_ref.at[use, 1 - pair],
            pair_in.at[use],
            pair_send.at[use],
            pair_recv.at[use],
            other,
        )
        for use in range(2)
    ]

    packing = pack_matrix(peers, tokens)
    unpacking = [unpack_matrix(peers, tokens, third) for third in range(3)]
    clean_scale, noise_scale = scale_ref[0], scale_ref[1]

    state = clean_scale * latent_ref[...].astype(F32) + noise_scale * noise_ref[...].astype(F32)
    center = state - jnp.mean(state, axis=1, keepdims=True)
    inv_std = lax.rsqrt(jnp.mean(center * center, axis=1, keepdims=True) + norm_eps)
    input_one[...] = (center * inv_std).astype(BF)
    for load in loads[0]:
        load.wait()
    qkv_one[...] = dot_nt(input_one[...], weights_ref[0, : 3 * LANES]).astype(BF)
    attend_forward(heads, qkv_one, probs_one, attn_one, None)

    def fill(use, rows_ref, weights):
        def both(*blocks):
            sources = [
                rows_ref[pl.ds(pl.multiple_of(block * quarter, quarter), quarter), :]
                for block in blocks
            ]
            result = dot(jnp.concatenate(sources, axis=0), weights)
            for place, block in enumerate(blocks):
                sum_blocks[use, block] = result[place * quarter : (place + 1) * quarter].astype(BF)

        return both

    pl.semaphore_wait(barrier, peers + 3)
    ring_sums[0].start(fill(0, attn_one, weights_ref[0, 3 * LANES :]))

    mine = pl.ds(pl.multiple_of(x * quarter, quarter), quarter)
    first_out[...] = jnp.concatenate(
        [
            pack(latent_ref[mine, :], packing, peers),
            pack(noise_ref[mine, :], packing, peers),
        ],
        axis=1,
    ).astype(BF)
    first.start()

    ring_sums[0].middle()
    out_one = ring_sums[0].finish()

    swap_out[0] = pack(out_one.astype(BF), packing, peers).astype(BF)
    swaps[0].start()
    first.finish()
    messages = first_in[...].astype(F32)
    clean = unpack(messages[:, :8], unpacking, peers)
    noise_pos[...] = unpack(messages[:, 8:], unpacking, peers)
    start_pos[...] = clean_scale * clean + noise_scale * noise_pos[...]
    swaps[0].finish()
    state = start_pos[...] + unpack(swap_in[0].astype(F32), unpacking, peers)
    state_ref[...] = state
    center = state - jnp.mean(state, axis=1, keepdims=True)
    inv_two = lax.rsqrt(jnp.mean(center * center, axis=1, keepdims=True) + norm_eps)
    norm_ref[...] = center * inv_two
    gather_blocks[0, x] = norm_ref[...].astype(BF)
    gathers[0].start()
    gathers[0].middle()

    for load in loads[1]:
        load.wait()
    row, col = iota((rows, rows), 0), iota((rows, rows), 1)
    same = (row // quarter == col // quarter) & (row % tokens == col % tokens)
    gathers[0].project(weights_ref[1, : 3 * LANES], qkv_two)
    attend_forward(heads, qkv_two, probs_two, attn_two, same)
    ring_sums[1].start(fill(1, attn_two, weights_ref[1, 3 * LANES :]))
    ring_sums[1].middle()
    diff = state_ref[...] + ring_sums[1].finish() - noise_pos[...]
    error = jnp.sum(jnp.sum(diff * diff, axis=1, keepdims=True), axis=0, keepdims=True)
    sign = 1.0 - 2.0 * pair.astype(F32)
    grad = diff * (2.0 * sign / width)
    grad_ref[...] = grad
    gather_blocks[1, x] = grad.astype(BF)
    gathers[1].start()
    gathers[1].middle()

    gathers[1].project(weights_ref[1, 3 * LANES :], dout_ref)
    attend_backward(heads, qkv_two, probs_two, dout_ref, dqkv_ref)
    ring_sums[2].start(fill(2, dqkv_ref, weights_ref[1, : 3 * LANES]))
    compact_ref[...] = compact(dqkv_ref)
    ring_sums[2].middle()

    def flat_view(use):
        return lambda start, size: gather_blocks[use, :, :, start : start + size].reshape(
            rows, size
        )

    class View:
        def __init__(self, use):
            self.read = flat_view(use)

        def __getitem__(self, index):
            lanes = index[1]
            return self.read(lanes.start, lanes.stop - lanes.start)

    weight_grads(View(0), compact_ref, View(1), attn_two, partial_ref.at[0], half_rows)
    pairs[0].start()
    dnorm = ring_sums[2].finish()
    normed = norm_ref[...]
    mean_grad = jnp.mean(dnorm, axis=1, keepdims=True)
    mean_prod = jnp.mean(dnorm * normed, axis=1, keepdims=True)
    dstate = grad_ref[...] + inv_two * (dnorm - mean_grad - normed * mean_prod)

    messages = pack(dstate.astype(BF), packing, peers)
    inner = iota(messages.shape, 1)
    error_high = error.astype(BF).astype(F32)
    error_low = error - error_high
    messages = jnp.where(inner == 6, error_high.reshape(1, 1, 1), messages)
    messages = jnp.where(inner == 7, error_low.reshape(1, 1, 1), messages)
    swap_out[1] = messages.astype(BF)
    swaps[1].start()

    def reduce_pair(use):
        pairs[use].wait()
        own = partial_ref[use, pair].astype(F32) + pair_in[use].astype(F32)
        y_blocks[use] = own.astype(BF).reshape(NY, y_rows, width)

    shape = (planes * z_rows, y_rows)
    row, col = iota(shape, 0), iota(shape, 1)
    spread = (row % z_rows < out_rows) & (col == (row // z_rows) * out_rows + row % z_rows)
    spread = spread.astype(F32).astype(BF)

    def start_z(use):
        rows_here = y_sums[use].finish().astype(BF)
        z_out[use] = dot(spread, rows_here).reshape(planes, z_rows, width).astype(BF)
        z_swaps[use].start()

    def finish_z(use):
        z_swaps[use].finish()
        return jnp.sum(z_in[use].astype(F32), axis=0)

    reduce_pair(0)
    y_sums[0].start()
    swaps[1].finish()
    messages = swap_in[1].astype(F32)
    gather_blocks[2, x] = unpack(messages, unpacking, peers).astype(BF)
    gathers[2].start()
    total = jnp.sum(messages, axis=0)
    err_x[x] = jnp.broadcast_to(total[6:7, :128] + total[7:8, :128], (8, 128))
    err_copies = [
        remote(
            err_x.at[x],
            err_x.at[x],
            err_x_send.at[offset - 1],
            err_x_recv.at[offset - 1],
            at_x((x + offset) % 4),
        )
        for offset in range(1, 4)
    ]
    for copy in err_copies:
        copy.start()
    gathers[2].middle()
    y_sums[0].middle()

    gathers[2].project(weights_ref[0, 3 * LANES :], dout_ref)
    for copy in err_copies:
        copy.wait()
    err_pair[pair] = jnp.sum(err_x[...], axis=0)
    err_copy = remote(err_pair.at[pair], err_pair.at[pair], err_pair_send, err_pair_recv, other)
    err_copy.start()
    attend_backward(heads, qkv_one, probs_one, dout_ref, dqkv_ref)
    compact_ref[...] = compact(dqkv_ref)
    weight_grads(input_one, compact_ref, View(2), attn_one, partial_ref.at[1], half_rows)
    pairs[1].start()
    start_z(0)
    reduce_pair(1)
    y_sums[1].start()
    err_copy.wait()
    margin = (err_pair[0] - err_pair[1]) * (1.0 / (rows * peers * width))
    scaled = beta_dpo * (margin - (ref_losses[0] - ref_losses[1]))
    loss = jnp.maximum(scaled, 0.0) + jnp.log1p(jnp.exp(-jnp.abs(scaled)))
    loss_out[0, 0] = loss[0, 0]
    factor = (rows * peers * beta_dpo) * jax.nn.sigmoid(scaled)
    factor = factor[:1, :1]
    y_sums[1].middle()
    grads_out[:, 1, :] = (finish_z(0) * factor)[:out_rows]
    start_z(1)
    grads_out[:, 0, :] = (finish_z(1) * factor)[:out_rows]


def local(latents, noise, timesteps, ref_losses, weights):
    width, columns = weights.shape[0], weights.shape[3]
    rows = latents.shape[2]
    peers = lax.axis_size("seq")
    quarter = rows // 4
    planes = peers // NY
    half_rows = width // 2
    y_rows = half_rows // NY
    y_cut = (y_rows // 32 + 1) * 16
    out_rows = y_rows // planes
    z_rows = -(-out_rows // 8) * 8
    heads = columns // HEAD_DIM

    angle = (timesteps[0, 0].astype(F32) / 1000.0 + 0.008) / 1.008 * (math.pi / 2)
    plan = jnp.cos(angle) ** 2
    scales = jnp.stack([jnp.sqrt(plan), jnp.sqrt(1.0 - plan)])

    vmem = pltpu.VMEM
    dma = pltpu.SemaphoreType.DMA
    third = width // 3
    grads, loss = pl.pallas_call(
        functools.partial(kernel, peers, heads),
        out_shape=(
            jax.ShapeDtypeStruct((out_rows, 2, width), F32),
            jax.ShapeDtypeStruct((1, 1), F32),
        ),
        in_specs=[
            pl.BlockSpec(memory_space=pltpu.SMEM),
            pl.BlockSpec(memory_space=pltpu.SMEM),
            pl.BlockSpec(memory_space=vmem),
            pl.BlockSpec(memory_space=vmem),
            pl.BlockSpec(memory_space=pl.ANY),
        ],
        out_specs=(pl.BlockSpec(memory_space=vmem), pl.BlockSpec(memory_space=pltpu.SMEM)),
        scratch_shapes=[
            vmem((2, 4 * LANES, width), BF),
            dma((2, 4)),
            vmem((rows, width), BF),
            vmem((rows, 3 * LANES), BF),
            vmem((rows, 3 * LANES), BF),
            vmem((heads, rows, rows), F32),
            vmem((heads, rows, rows), F32),
            vmem((rows, LANES), BF),
            vmem((rows, LANES), BF),
            vmem((rows, LANES), BF),
            vmem((rows, 3 * LANES), BF),
            vmem((rows, 896), BF),
            vmem((quarter, width), F32),
            vmem((quarter, width), F32),
            vmem((quarter, width), F32),
            vmem((quarter, width), F32),
            vmem((quarter, width), F32),
            vmem((3, 4, quarter, width), BF),
            vmem((3, 3, quarter // 2, width), BF),
            vmem((3, 3, quarter // 2, width), BF),
            dma((3, 6)),
            dma((3, 6)),
            vmem((3, 4, quarter, width), BF),
            dma((3, 6)),
            dma((3, 6)),
            vmem((peers, 16, third), BF),
            vmem((peers, 16, third), BF),
            vmem((2, peers, 8, third), BF),
            vmem((2, peers, 8, third), BF),
            dma((3,)),
            dma((3,)),
            vmem((2, 2, half_rows, width), BF),
            vmem((2, half_rows, width), BF),
            dma((2,)),
            dma((2,)),
            vmem((2, NY, y_rows, width), BF),
            vmem((2, 3, y_cut, width), BF),
            vmem((2, 3, y_rows - y_cut, width), BF),
            dma((2, 6)),
            dma((2, 6)),
            vmem((2, planes, z_rows, width), BF),
            vmem((2, planes, z_rows, width), BF),
            dma((2,)),
            dma((2,)),
            vmem((4, 8, 128), F32),
            dma((3,)),
            dma((3,)),
            vmem((2, 8, 128), F32),
            dma,
            dma,
        ],
        compiler_params=pltpu.CompilerParams(
            collective_id=0, has_side_effects=True, vmem_limit_bytes=60 * 2**20
        ),
    )(scales, ref_losses[:, 0], latents[0, 0], noise[0, 0], weights.transpose(1, 2, 3, 0))

    return (loss[0, 0], grads.reshape(out_rows, 2, 4, columns))


def solution(mesh):
    in_specs = (
        P("pair", None, "seq", None),
        P("pair", None, "seq", None),
        P("pair", None),
        P(),
        P(None, None, None, "tensor"),
    )
    out_specs = (P(), P(("pair", "seq"), None, None, "tensor"))
    return jax.shard_map(local, mesh=mesh, in_specs=in_specs, out_specs=out_specs, check_vma=False)
```

```python
import functools
import math

import jax
import jax.numpy as jnp
from jax import lax
from jax.experimental import pallas as pl
from jax.experimental.pallas import tpu as pltpu
from jax.sharding import PartitionSpec as P

HEAD_DIM = 72
LANES = 384
NY = 4
MESH = pl.DeviceIdType.MESH
BF = jnp.bfloat16
F32 = jnp.float32

beta_dpo = 0.5
norm_eps = 1e-06


def dot(a, b):
    return jnp.dot(a, b, preferred_element_type=F32)


def dot_nt(a, b):
    return lax.dot_general(a, b, (((1,), (1,)), ((), ())), preferred_element_type=F32)


def dot_tn(a, b):
    return lax.dot_general(a, b, (((0,), (0,)), ((), ())), preferred_element_type=F32)


def iota(shape, axis):
    return lax.broadcasted_iota(jnp.int32, shape, axis)


def head_mask(head, dtype):
    lane = iota((1, LANES), 1)
    return ((lane >= head * HEAD_DIM) & (lane < (head + 1) * HEAD_DIM)).astype(dtype)


def attend_forward(heads, qkv_ref, probs_ref, out_ref, mask):
    queries = qkv_ref[:, :LANES]
    keys = qkv_ref[:, LANES : 2 * LANES]
    values = qkv_ref[:, 2 * LANES :]
    total = None
    for head in range(heads):
        scores = dot_nt(queries * head_mask(head, BF), keys) * (HEAD_DIM**-0.5)
        if mask is not None:
            scores = jnp.where(mask, scores, -1e30)
        scores = jnp.exp(scores - jnp.max(scores, axis=1, keepdims=True))
        probs = scores * (1.0 / jnp.sum(scores, axis=1, keepdims=True))
        probs_ref[head] = probs
        part = dot(probs.astype(BF), values) * head_mask(head, F32)
        total = part if total is None else total + part
    out_ref[...] = total.astype(BF)


def values_backward(heads, probs_ref, grad_ref, dqkv_ref):
    grad = grad_ref[...]
    total = None
    for head in range(heads):
        part = dot_tn(probs_ref[head].astype(BF), grad) * head_mask(head, F32)
        total = part if total is None else total + part
    dqkv_ref[:, 2 * LANES :] = total.astype(BF)


def scores_backward(heads, qkv_ref, probs_ref, grad_ref, dqkv_ref):
    queries = qkv_ref[:, :LANES]
    keys = qkv_ref[:, LANES : 2 * LANES]
    values = qkv_ref[:, 2 * LANES :]
    grad = grad_ref[...]
    sums = [None, None]
    for head in range(heads):
        probs = probs_ref[head]
        dprobs = dot_nt(grad * head_mask(head, BF), values)
        delta = jnp.sum(dprobs * probs, axis=1, keepdims=True)
        dscores = (probs * (dprobs - delta) * (HEAD_DIM**-0.5)).astype(BF)
        parts = (dot(dscores, keys), dot_tn(dscores, queries))
        for slot in range(2):
            part = parts[slot] * head_mask(head, F32)
            sums[slot] = part if sums[slot] is None else sums[slot] + part
    for slot in range(2):
        dqkv_ref[:, slot * LANES : (slot + 1) * LANES] = sums[slot].astype(BF)


def beside(first, second):
    return jnp.concatenate(
        [first[:, :256], first[:, 256:] + second[:, :128], second[:, 128:]], axis=1
    )


def shifted(values, lanes):
    return pltpu.roll(values.astype(F32), lanes, 1)


def store_rows(out_ref, start, rows, half_rows):
    done, count = 0, rows.shape[0]
    while done < count:
        half, at = divmod(start + done, half_rows)
        size = min(count - done, half_rows - at)
        out_ref[half, at : at + size, :] = rows[done : done + size].astype(BF)
        done += size


def pack_matrix(peers, tokens):
    shape = (8 * peers, 3 * peers * tokens)
    row, col = iota(shape, 0), iota(shape, 1)
    peer, inner = row // 8, row % 8
    source = (inner // tokens) * (peers * tokens) + peer * tokens + inner % tokens
    return ((inner < 3 * tokens) & (col == source)).astype(F32).astype(BF)


def unpack_matrix(peers, tokens, third):
    shape = (peers * tokens, 8 * peers)
    token, col = iota(shape, 0), iota(shape, 1)
    source = (token // tokens) * 8 + third * tokens + token % tokens
    return (col == source).astype(F32).astype(BF)


def pack(rows, matrix, peers):
    third = rows.shape[1] // 3
    stacked = jnp.concatenate(
        [rows[:, :third], rows[:, third : 2 * third], rows[:, 2 * third :]], axis=0
    )
    return dot(matrix, stacked).reshape(peers, 8, third)


def unpack(messages, matrices, peers):
    flat = messages.reshape(8 * peers, messages.shape[2]).astype(BF)
    return jnp.concatenate([dot(matrix, flat) for matrix in matrices], axis=1)


def remote(src, dst, send, recv, device):
    return pltpu.make_async_remote_copy(
        src_ref=src,
        dst_ref=dst,
        send_sem=send,
        recv_sem=recv,
        device_id=device,
        device_id_type=MESH,
    )


def halves(rows):
    unit = 16 if rows >= 64 else rows // 4
    cut = -(-rows // (2 * unit)) * unit
    low, high = -(-cut // (2 * unit)) * unit, -(-(rows - cut) // (2 * unit)) * unit
    return (
        cut,
        ((0, low), (low, cut - low)),
        ((cut, high), (cut + high, rows - cut - high)),
    )


class RingGather:
    def __init__(self, blocks, send, recv, me, device):
        self.blocks, self.me = blocks, me
        self.right, self.left = (me + 1) % 4, (me + 3) % 4
        self.opposite = (me + 2) % 4
        rows = blocks.shape[1]
        cut, lows, highs = halves(rows)
        right, left = device(self.right), device(self.left)

        def copy(block, piece, index, to):
            ref = blocks.at[block, pl.ds(*piece)]
            return remote(ref, ref, send.at[index], recv.at[index], to)

        self.first, self.passes = [], []
        for place, piece in enumerate(lows):
            self.first.append(copy(me, piece, place, right))
            self.passes.append(copy(self.left, piece, 4 + place, right))
        for place, piece in enumerate(highs):
            self.first.append(copy(me, piece, 2 + place, left))
            self.passes.append(copy(self.right, piece, 6 + place, left))
        self.next_right = copy(me, (cut, rows - cut), 8, right)
        self.next_left = copy(me, (0, cut), 9, left)

    def start(self):
        for place in (0, 2, 1, 3):
            self.first[place].start()
        self.next_right.start()
        self.next_left.start()

    def middle(self):
        for place in (0, 2, 1, 3):
            self.first[place].wait_recv()
            self.passes[place].start()

    def project(self, weights, out_ref):
        size = self.blocks.shape[1]
        self.next_right.wait_recv()
        self.next_left.wait_recv()
        near = (self.me, self.left, self.right)
        result = dot_nt(jnp.concatenate([self.blocks[block] for block in near], axis=0), weights)
        for place, block in enumerate(near):
            out_ref[pl.ds(pl.multiple_of(block * size, size), size), :] = result[
                place * size : (place + 1) * size
            ].astype(BF)
        for copy in self.passes:
            copy.wait_recv()
        out_ref[pl.ds(pl.multiple_of(self.opposite * size, size), size), :] = dot_nt(
            self.blocks[self.opposite], weights
        ).astype(BF)
        for copy in self.first + self.passes + [self.next_right, self.next_left]:
            copy.wait_send()


class Exchange:
    def __init__(self, out, into, send, recv, me, peers):
        self.out, self.into, self.me, self.peers = out, into, me, peers
        self.copies = [
            remote(out.at[peer], into.at[me], send, recv, device) for peer, device in peers
        ]
        every = pl.ds(0, len(peers))
        self.all = remote(out.at[every], into.at[every], send, recv, peers[0][1])

    def start(self):
        for copy in self.copies:
            copy.start()

    def keep(self):
        self.into[self.me] = self.out[self.me]

    def finish(self):
        self.all.wait()


class Total:
    def __init__(self, refs, pair, other, y, y_peers, z, z_peers):
        self.partial, self.pair_in, y_out, y_in, z_out, z_in, sems = refs
        self.pair = pair
        self.swap = remote(self.partial.at[1 - pair], self.pair_in, sems.at[0], sems.at[1], other)
        self.over_y = Exchange(y_out, y_in, sems.at[2], sems.at[3], y, y_peers)
        self.over_z = Exchange(z_out, z_in, sems.at[4], sems.at[5], z, z_peers)

    def start(self):
        self.swap.start()

    def start_y(self):
        self.swap.wait()
        step = self.over_y
        rows = step.out.shape[1]

        def fill(block):
            at = pl.ds(pl.multiple_of(block * rows, 16), rows)
            own = self.partial[self.pair, at, :].astype(F32) + self.pair_in[at, :].astype(F32)
            step.out[block] = own.astype(BF)

        for (block, _), copy in zip(step.peers, step.copies):
            fill(block)
            copy.start()
        fill(step.me)
        step.keep()

    def start_z(self, spread):
        self.over_y.finish()
        rows = jnp.sum(self.over_y.into[...].astype(F32), axis=0).astype(BF)
        step = self.over_z
        step.out[...] = dot(spread, rows).reshape(step.out.shape).astype(BF)
        step.start()
        step.keep()

    def finish(self):
        self.over_z.finish()
        return jnp.sum(self.over_z.into[...].astype(F32), axis=0)


def kernel(
    peers,
    heads,
    scale_ref,
    ref_losses,
    latent_ref,
    noise_ref,
    weights_hbm,
    grads_out,
    loss_out,
    weights_ref,
    weights_sem,
    input_one,
    qkv_one,
    qkv_two,
    probs_one,
    probs_two,
    attn_one,
    attn_two,
    dout_ref,
    dqkv_ref,
    start_pos,
    noise_pos,
    state_ref,
    norm_ref,
    grad_ref,
    sum_out,
    sum_in,
    sum_send,
    sum_recv,
    gather_blocks,
    gather_send,
    gather_recv,
    first_out,
    first_in,
    swap_out,
    swap_in,
    swap_send,
    swap_recv,
    err_x,
    err_x_send,
    err_x_recv,
    err_pair,
    err_pair_send,
    err_pair_recv,
    *total_refs,
):
    pair, seq, x = lax.axis_index("pair"), lax.axis_index("seq"), lax.axis_index("tensor")
    planes = peers // NY
    y, z = seq // planes, seq % planes
    rows, width = latent_ref.shape
    quarter = rows // 4
    tokens = quarter // peers
    half_rows = width // 2
    y_rows = half_rows // NY
    out_rows = y_rows // planes
    z_rows = total_refs[4].shape[1]

    def at_x(index):
        return (pair, seq, index)

    def at_y(index):
        return (pair, index * planes + z, x)

    def at_z(index):
        return (pair, y * planes + index, x)

    def at_seq(index):
        return (pair, index, x)

    other = (1 - pair, seq, x)

    columns = weights_hbm.shape[2]
    loads = [
        [
            pltpu.make_async_copy(
                weights_hbm.at[block, slot],
                weights_ref.at[block, pl.ds(slot * LANES, columns)],
                weights_sem.at[block, slot],
            )
            for slot in range(4)
        ]
        for block in range(2)
    ]
    for load in loads[0] + loads[1]:
        load.start()
    for slot in range(4):
        for block in range(2):
            weights_ref[block, slot * LANES + columns : (slot + 1) * LANES, :] = jnp.zeros(
                (LANES - columns, width), BF
            )

    barrier = pltpu.get_barrier_semaphore()

    def greet(offset, carry):
        pl.semaphore_signal(
            barrier, inc=1, device_id=at_seq((seq + offset) % peers), device_id_type=MESH
        )
        return carry

    lax.fori_loop(1, peers, greet, 0)
    for offset in range(1, 4):
        pl.semaphore_signal(
            barrier, inc=1, device_id=at_x((x + offset) % 4), device_id_type=MESH
        )
    pl.semaphore_signal(barrier, inc=1, device_id=other, device_id_type=MESH)

    def hops(offset, count):
        return min(offset, count - offset)

    x_peers = [((x + offset) % 4, at_x((x + offset) % 4)) for offset in (2, 1, 3)]
    y_peers = [((y + offset) % NY, at_y((y + offset) % NY)) for offset in (2, 1, 3)]
    z_order = sorted(range(1, planes), key=lambda offset: -hops(offset, planes))
    z_peers = [((z + offset) % planes, at_z((z + offset) % planes)) for offset in z_order]
    order = sorted(
        ((dy, dz) for dy in range(NY) for dz in range(planes) if dy or dz),
        key=lambda offset: -hops(offset[0], NY) - hops(offset[1], planes),
    )
    seq_peers = []
    for dy, dz in order:
        peer = ((y + dy) % NY) * planes + (z + dz) % planes
        seq_peers.append((peer, at_seq(peer)))

    sums = [
        Exchange(
            sum_out.at[use], sum_in.at[use], sum_send.at[use], sum_recv.at[use], x, x_peers
        )
        for use in range(3)
    ]
    gathers = [
        RingGather(gather_blocks.at[use], gather_send.at[use], gather_recv.at[use], x, at_x)
        for use in range(3)
    ]
    first = Exchange(first_out, first_in, swap_send.at[0], swap_recv.at[0], seq, seq_peers)
    swaps = [
        Exchange(
            swap_out.at[use],
            swap_in.at[use],
            swap_send.at[use + 1],
            swap_recv.at[use + 1],
            seq,
            seq_peers,
        )
        for use in range(2)
    ]
    total_two, total_values, total_queries, total_keys = [
        Total(total_refs[7 * use : 7 * use + 7], pair, other, y, y_peers, z, z_peers)
        for use in range(4)
    ]

    packing = pack_matrix(peers, tokens)
    unpacking = [unpack_matrix(peers, tokens, third) for third in range(3)]
    clean_scale, noise_scale = scale_ref[0], scale_ref[1]

    state = clean_scale * latent_ref[...].astype(F32) + noise_scale * noise_ref[...].astype(F32)
    center = state - jnp.mean(state, axis=1, keepdims=True)
    inv_std = lax.rsqrt(jnp.mean(center * center, axis=1, keepdims=True) + norm_eps)
    input_one[...] = (center * inv_std).astype(BF)
    for load in loads[0]:
        load.wait()
    qkv_one[...] = dot_nt(input_one[...], weights_ref[0, : 3 * LANES]).astype(BF)
    attend_forward(heads, qkv_one, probs_one, attn_one, None)

    def sum_start(use, rows_ref, weights):
        step = sums[use]
        (opposite, _), (right, _), (left, _) = step.peers
        for blocks in ((opposite, right), (left, x)):
            sources = [
                rows_ref[pl.ds(pl.multiple_of(block * quarter, quarter), quarter), :]
                for block in blocks
            ]
            result = dot(jnp.concatenate(sources, axis=0), weights)
            for place, block in enumerate(blocks):
                step.out[block] = result[place * quarter : (place + 1) * quarter].astype(BF)
            if blocks[0] is opposite:
                step.copies[0].start()
                step.copies[1].start()
            else:
                step.copies[2].start()

    def sum_finish(use):
        step = sums[use]
        step.finish()
        total = step.out[x].astype(F32)
        for peer, _ in step.peers:
            total = total + step.into[peer].astype(F32)
        return total

    pl.semaphore_wait(barrier, peers + 3)
    sum_start(0, attn_one, weights_ref[0, 3 * LANES :])

    mine = pl.ds(pl.multiple_of(x * quarter, quarter), quarter)
    first_out[...] = jnp.concatenate(
        [
            pack(latent_ref[mine, :], packing, peers),
            pack(noise_ref[mine, :], packing, peers),
        ],
        axis=1,
    ).astype(BF)
    first.start()
    first.keep()

    out_one = sum_finish(0)

    swap_out[0] = pack(out_one.astype(BF), packing, peers).astype(BF)
    swaps[0].start()
    swaps[0].keep()
    first.finish()
    messages = first_in[...].astype(F32)
    clean = unpack(messages[:, :8], unpacking, peers)
    noise_pos[...] = unpack(messages[:, 8:], unpacking, peers)
    start_pos[...] = clean_scale * clean + noise_scale * noise_pos[...]
    swaps[0].finish()
    state = start_pos[...] + unpack(swap_in[0].astype(F32), unpacking, peers)
    state_ref[...] = state
    center = state - jnp.mean(state, axis=1, keepdims=True)
    inv_two = lax.rsqrt(jnp.mean(center * center, axis=1, keepdims=True) + norm_eps)
    norm_ref[...] = center * inv_two
    gather_blocks[0, x] = norm_ref[...].astype(BF)
    gathers[0].start()
    gathers[0].middle()

    for load in loads[1]:
        load.wait()
    row, col = iota((rows, rows), 0), iota((rows, rows), 1)
    same = (row // quarter == col // quarter) & (row % tokens == col % tokens)
    gathers[0].project(weights_ref[1, : 3 * LANES], qkv_two)
    attend_forward(heads, qkv_two, probs_two, attn_two, same)
    sum_start(1, attn_two, weights_ref[1, 3 * LANES :])
    diff = state_ref[...] + sum_finish(1) - noise_pos[...]
    error = jnp.sum(jnp.sum(diff * diff, axis=1, keepdims=True), axis=0, keepdims=True)
    sign = 1.0 - 2.0 * pair.astype(F32)
    grad = diff * (2.0 * sign / width)
    grad_ref[...] = grad
    gather_blocks[1, x] = grad.astype(BF)
    gathers[1].start()
    gathers[1].middle()

    gathers[1].project(weights_ref[1, 3 * LANES :], dout_ref)
    scores_backward(heads, qkv_two, probs_two, dout_ref, dqkv_ref)
    values_backward(heads, probs_two, dout_ref, dqkv_ref)
    sum_start(2, dqkv_ref, weights_ref[1, : 3 * LANES])

    def view(use, start, size):
        return gather_blocks[use, :, :, start : start + size].reshape(rows, size)

    step = 128
    shifted_keys = shifted(dqkv_ref[:, LANES : 2 * LANES], 32)
    shifted_values = shifted(dqkv_ref[:, 2 * LANES :], 64)
    queries_keys = beside(dqkv_ref[:, :LANES].astype(F32), shifted_keys)
    dqkv = jnp.concatenate(
        [
            queries_keys[:, :512],
            queries_keys[:, 512:] + shifted_values[:, :128],
            shifted_values[:, 128:],
        ],
        axis=1,
    ).astype(BF)
    attn = shifted(attn_two[...], 96).astype(BF)
    for start in range(0, width, step):
        first_part = dot_tn(view(0, start, step), dqkv)
        second_part = dot_tn(view(1, start, step), attn)
        block = jnp.concatenate(
            [
                first_part[:, :768],
                first_part[:, 768:] + second_part[:, :128],
                second_part[:, 128:],
            ],
            axis=1,
        )
        store_rows(total_two.partial, start, block, half_rows)
    total_two.start()
    dnorm = sum_finish(2)
    normed = norm_ref[...]
    mean_grad = jnp.mean(dnorm, axis=1, keepdims=True)
    mean_prod = jnp.mean(dnorm * normed, axis=1, keepdims=True)
    dstate = grad_ref[...] + inv_two * (dnorm - mean_grad - normed * mean_prod)

    messages = pack(dstate.astype(BF), packing, peers)
    inner = iota(messages.shape, 1)
    error_high = error.astype(BF).astype(F32)
    error_low = error - error_high
    messages = jnp.where(inner == 6, error_high.reshape(1, 1, 1), messages)
    messages = jnp.where(inner == 7, error_low.reshape(1, 1, 1), messages)
    swap_out[1] = messages.astype(BF)
    swaps[1].start()
    swaps[1].keep()

    shape = (planes * z_rows, y_rows)
    row, col = iota(shape, 0), iota(shape, 1)
    spread = (row % z_rows < out_rows) & (col == (row // z_rows) * out_rows + row % z_rows)
    spread = spread.astype(F32).astype(BF)

    total_two.start_y()
    swaps[1].finish()
    messages = swap_in[1].astype(F32)
    gather_blocks[2, x] = unpack(messages, unpacking, peers).astype(BF)
    gathers[2].start()
    total = jnp.sum(messages, axis=0)
    err_x[x] = jnp.broadcast_to(total[6:7, :128] + total[7:8, :128], (8, 128))
    err_copies = [
        remote(
            err_x.at[x],
            err_x.at[x],
            err_x_send.at[offset - 1],
            err_x_recv.at[offset - 1],
            at_x((x + offset) % 4),
        )
        for offset in range(1, 4)
    ]
    for copy in err_copies:
        copy.start()
    gathers[2].middle()

    gathers[2].project(weights_ref[0, 3 * LANES :], dout_ref)
    values_backward(heads, probs_one, dout_ref, dqkv_ref)
    values = dqkv_ref[:, 2 * LANES :]
    attn = shifted(attn_one[...], 32).astype(BF)
    for start in range(0, width, step):
        block = beside(
            dot_tn(input_one[:, start : start + step], values),
            dot_tn(view(2, start, step), attn),
        )
        store_rows(total_values.partial, start, block, half_rows)
    total_values.start()
    total_two.start_z(spread)
    for copy in err_copies:
        copy.wait()
    err_pair[pair] = jnp.sum(err_x[...], axis=0)
    err_copy = remote(err_pair.at[pair], err_pair.at[pair], err_pair_send, err_pair_recv, other)
    err_copy.start()
    total_values.start_y()
    scores_backward(heads, qkv_one, probs_one, dout_ref, dqkv_ref)
    queries_keys = beside(
        dqkv_ref[:, :LANES].astype(F32), shifted(dqkv_ref[:, LANES : 2 * LANES], 32)
    ).astype(BF)
    for start in range(0, width, step):
        block = dot_tn(input_one[:, start : start + step], queries_keys)
        store_rows(total_queries.partial, start, block[:, :LANES], half_rows)
        store_rows(total_keys.partial, start, block[:, LANES:], half_rows)
    total_queries.start()
    total_keys.start()
    err_copy.wait()
    margin = (err_pair[0] - err_pair[1]) * (1.0 / (rows * peers * width))
    scaled = beta_dpo * (margin - (ref_losses[0] - ref_losses[1]))
    loss = jnp.maximum(scaled, 0.0) + jnp.log1p(jnp.exp(-jnp.abs(scaled)))
    loss_out[0, 0] = loss[0, 0]
    factor = (rows * peers * beta_dpo) * jax.nn.sigmoid(scaled)
    factor = factor[:1, :1]
    total_queries.start_y()
    total_keys.start_y()
    grads_out[:, 1, :] = (total_two.finish() * factor)[:out_rows]
    total_values.start_z(spread)
    total_queries.start_z(spread)
    total_keys.start_z(spread)
    values_output = pltpu.roll(total_values.finish(), 64, 1)
    queries = total_queries.finish()
    keys = total_keys.finish()
    grads = jnp.concatenate(
        [
            queries,
            keys[:, :128],
            keys[:, 128:] + values_output[:, :128],
            values_output[:, 128:],
        ],
        axis=1,
    )
    grads_out[:, 0, :] = (grads * factor)[:out_rows]


def local(latents, noise, timesteps, ref_losses, weights):
    width, columns = weights.shape[0], weights.shape[3]
    rows = latents.shape[2]
    peers = lax.axis_size("seq")
    quarter = rows // 4
    planes = peers // NY
    half_rows = width // 2
    y_rows = half_rows // NY
    out_rows = y_rows // planes
    z_rows = -(-out_rows // 8) * 8
    heads = columns // HEAD_DIM

    angle = (timesteps[0, 0].astype(F32) / 1000.0 + 0.008) / 1.008 * (math.pi / 2)
    plan = jnp.cos(angle) ** 2
    scales = jnp.stack([jnp.sqrt(plan), jnp.sqrt(1.0 - plan)])

    vmem = pltpu.VMEM
    dma = pltpu.SemaphoreType.DMA
    third = width // 3
    totals = []
    for lanes in (width, 640, LANES, 256):
        totals += [
            vmem((2, half_rows, lanes), BF),
            vmem((half_rows, lanes), BF),
            vmem((NY, y_rows, lanes), BF),
            vmem((NY, y_rows, lanes), BF),
            vmem((planes, z_rows, lanes), BF),
            vmem((planes, z_rows, lanes), BF),
            dma((6,)),
        ]
    grads, loss = pl.pallas_call(
        functools.partial(kernel, peers, heads),
        out_shape=(
            jax.ShapeDtypeStruct((out_rows, 2, width), F32),
            jax.ShapeDtypeStruct((1, 1), F32),
        ),
        in_specs=[
            pl.BlockSpec(memory_space=pltpu.SMEM),
            pl.BlockSpec(memory_space=pltpu.SMEM),
            pl.BlockSpec(memory_space=vmem),
            pl.BlockSpec(memory_space=vmem),
            pl.BlockSpec(memory_space=pl.ANY),
        ],
        out_specs=(pl.BlockSpec(memory_space=vmem), pl.BlockSpec(memory_space=pltpu.SMEM)),
        scratch_shapes=[
            vmem((2, 4 * LANES, width), BF),
            dma((2, 4)),
            vmem((rows, width), BF),
            vmem((rows, 3 * LANES), BF),
            vmem((rows, 3 * LANES), BF),
            vmem((heads, rows, rows), F32),
            vmem((heads, rows, rows), F32),
            vmem((rows, LANES), BF),
            vmem((rows, LANES), BF),
            vmem((rows, LANES), BF),
            vmem((rows, 3 * LANES), BF),
            vmem((quarter, width), F32),
            vmem((quarter, width), F32),
            vmem((quarter, width), F32),
            vmem((quarter, width), F32),
            vmem((quarter, width), F32),
            vmem((3, 4, quarter, width), BF),
            vmem((3, 4, quarter, width), BF),
            dma((3,)),
            dma((3,)),
            vmem((3, 4, quarter, width), BF),
            dma((3, 10)),
            dma((3, 10)),
            vmem((peers, 16, third), BF),
            vmem((peers, 16, third), BF),
            vmem((2, peers, 8, third), BF),
            vmem((2, peers, 8, third), BF),
            dma((3,)),
            dma((3,)),
            vmem((4, 8, 128), F32),
            dma((3,)),
            dma((3,)),
            vmem((2, 8, 128), F32),
            dma,
            dma,
            *totals,
        ],
        compiler_params=pltpu.CompilerParams(
            collective_id=0, has_side_effects=True, vmem_limit_bytes=60 * 2**20
        ),
    )(scales, ref_losses[:, 0], latents[0, 0], noise[0, 0], weights.transpose(1, 2, 3, 0))

    return (loss[0, 0], grads.reshape(out_rows, 2, 4, columns))


def solution(mesh):
    in_specs = (
        P("pair", None, "seq", None),
        P("pair", None, "seq", None),
        P("pair", None),
        P(),
        P(None, None, None, "tensor"),
    )
    out_specs = (P(), P(("pair", "seq"), None, None, "tensor"))
    return jax.shard_map(local, mesh=mesh, in_specs=in_specs, out_specs=out_specs, check_vma=False)
```

```python
import functools
import math

import jax
import jax.numpy as jnp
from jax import lax
from jax.experimental import pallas as pl
from jax.experimental.pallas import tpu as pltpu
from jax.sharding import PartitionSpec as P

HEAD_DIM = 72
LANES = 384
NY = 4
MESH = pl.DeviceIdType.MESH
BF = jnp.bfloat16
F32 = jnp.float32

beta_dpo = 0.5
norm_eps = 1e-06


def dot(a, b):
    return jnp.dot(a, b, preferred_element_type=F32)


def dot_nt(a, b):
    return lax.dot_general(a, b, (((1,), (1,)), ((), ())), preferred_element_type=F32)


def dot_tn(a, b):
    return lax.dot_general(a, b, (((0,), (0,)), ((), ())), preferred_element_type=F32)


def iota(shape, axis):
    return lax.broadcasted_iota(jnp.int32, shape, axis)


def head_mask(head, dtype):
    lane = iota((1, LANES), 1)
    return ((lane >= head * HEAD_DIM) & (lane < (head + 1) * HEAD_DIM)).astype(dtype)


def attend_forward(heads, qkv_ref, probs_ref, out_ref, mask):
    queries = qkv_ref[:, :LANES]
    keys = qkv_ref[:, LANES : 2 * LANES]
    values = qkv_ref[:, 2 * LANES :]
    total = None
    for head in range(heads):
        scores = dot_nt(queries * head_mask(head, BF), keys) * (HEAD_DIM**-0.5)
        if mask is not None:
            scores = jnp.where(mask, scores, -1e30)
        scores = jnp.exp(scores - jnp.max(scores, axis=1, keepdims=True))
        probs = scores * (1.0 / jnp.sum(scores, axis=1, keepdims=True))
        probs_ref[head] = probs
        part = dot(probs.astype(BF), values) * head_mask(head, F32)
        total = part if total is None else total + part
    out_ref[...] = total.astype(BF)


def values_backward(heads, probs_ref, grad_ref, dqkv_ref):
    grad = grad_ref[...]
    total = None
    for head in range(heads):
        part = dot_tn(probs_ref[head].astype(BF), grad) * head_mask(head, F32)
        total = part if total is None else total + part
    dqkv_ref[:, 2 * LANES :] = total.astype(BF)


def scores_backward(heads, qkv_ref, probs_ref, grad_ref, dqkv_ref):
    queries = qkv_ref[:, :LANES]
    keys = qkv_ref[:, LANES : 2 * LANES]
    values = qkv_ref[:, 2 * LANES :]
    grad = grad_ref[...]
    sums = [None, None]
    for head in range(heads):
        probs = probs_ref[head]
        dprobs = dot_nt(grad * head_mask(head, BF), values)
        delta = jnp.sum(dprobs * probs, axis=1, keepdims=True)
        dscores = (probs * (dprobs - delta) * (HEAD_DIM**-0.5)).astype(BF)
        parts = (dot(dscores, keys), dot_tn(dscores, queries))
        for slot in range(2):
            part = parts[slot] * head_mask(head, F32)
            sums[slot] = part if sums[slot] is None else sums[slot] + part
    for slot in range(2):
        dqkv_ref[:, slot * LANES : (slot + 1) * LANES] = sums[slot].astype(BF)


def beside(first, second):
    return jnp.concatenate(
        [first[:, :256], first[:, 256:] + second[:, :128], second[:, 128:]], axis=1
    )


def shifted(values, lanes):
    return pltpu.roll(values.astype(F32), lanes, 1)


def store_rows(out_ref, start, rows, half_rows):
    done, count = 0, rows.shape[0]
    while done < count:
        half, at = divmod(start + done, half_rows)
        size = min(count - done, half_rows - at)
        out_ref[half, at : at + size, :] = rows[done : done + size].astype(BF)
        done += size


def selection(source, columns):
    col = iota((source.shape[0], columns), 1)
    return (col == source).astype(F32).astype(BF)


def pack_matrix(peers, tokens):
    row = iota((8 * peers, 1), 0)
    peer, inner = row // 8, row % 8
    source = (inner // tokens) * (peers * tokens) + peer * tokens + inner % tokens
    return selection(jnp.where(inner < 3 * tokens, source, -1), 3 * peers * tokens)


def unpack_matrix(peers, tokens, third):
    token = iota((peers * tokens, 1), 0)
    source = (token // tokens) * 8 + third * tokens + token % tokens
    return selection(source, 8 * peers)


def pack(rows, matrix, peers):
    third = rows.shape[1] // 3
    stacked = jnp.concatenate(
        [rows[:, :third], rows[:, third : 2 * third], rows[:, 2 * third :]], axis=0
    )
    return dot(matrix, stacked).reshape(peers, 8, third)


def unpack(messages, matrices, peers):
    flat = messages.reshape(8 * peers, messages.shape[2]).astype(BF)
    return jnp.concatenate([dot(matrix, flat) for matrix in matrices], axis=1)


def remote(src, dst, send, recv, device):
    return pltpu.make_async_remote_copy(
        src_ref=src,
        dst_ref=dst,
        send_sem=send,
        recv_sem=recv,
        device_id=device,
        device_id_type=MESH,
    )


def halves(rows):
    unit = 16 if rows >= 64 else rows // 4
    cut = -(-rows // (2 * unit)) * unit
    low, high = -(-cut // (2 * unit)) * unit, -(-(rows - cut) // (2 * unit)) * unit
    return (
        cut,
        ((0, low), (low, cut - low)),
        ((cut, high), (cut + high, rows - cut - high)),
    )


class RingGather:
    def __init__(self, blocks, send, recv, me, device):
        self.blocks, self.me = blocks, me
        self.right, self.left = (me + 1) % 4, (me + 3) % 4
        self.opposite = (me + 2) % 4
        rows = blocks.shape[1]
        cut, lows, highs = halves(rows)
        right, left = device(self.right), device(self.left)

        def copy(block, piece, index, to):
            ref = blocks.at[block, pl.ds(*piece)]
            return remote(ref, ref, send.at[index], recv.at[index], to)

        self.first, self.passes = [], []
        for place, piece in enumerate(lows):
            self.first.append(copy(me, piece, place, right))
            self.passes.append(copy(self.left, piece, 4 + place, right))
        for place, piece in enumerate(highs):
            self.first.append(copy(me, piece, 2 + place, left))
            self.passes.append(copy(self.right, piece, 6 + place, left))
        self.next_right = copy(me, (cut, rows - cut), 8, right)
        self.next_left = copy(me, (0, cut), 9, left)

    def start(self):
        for place in (0, 2, 1, 3):
            self.first[place].start()
        self.next_right.start()
        self.next_left.start()

    def middle(self):
        for place in (0, 2, 1, 3):
            self.first[place].wait_recv()
            self.passes[place].start()

    def project(self, weights, out_ref):
        size = self.blocks.shape[1]
        self.next_right.wait_recv()
        self.next_left.wait_recv()
        near = (self.me, self.left, self.right)
        result = dot_nt(jnp.concatenate([self.blocks[block] for block in near], axis=0), weights)
        for place, block in enumerate(near):
            out_ref[pl.ds(pl.multiple_of(block * size, size), size), :] = result[
                place * size : (place + 1) * size
            ].astype(BF)
        for copy in self.passes:
            copy.wait_recv()
        out_ref[pl.ds(pl.multiple_of(self.opposite * size, size), size), :] = dot_nt(
            self.blocks[self.opposite], weights
        ).astype(BF)
        for copy in self.first + self.passes + [self.next_right, self.next_left]:
            copy.wait_send()


class Exchange:
    def __init__(self, out, into, send, recv, me, peers):
        self.out, self.into, self.me, self.peers = out, into, me, peers
        self.copies = [
            remote(out.at[peer], into.at[me], send, recv, device) for peer, device in peers
        ]
        every = pl.ds(0, len(peers))
        self.all = remote(out.at[every], into.at[every], send, recv, peers[0][1])

    def start(self):
        for copy in self.copies:
            copy.start()

    def keep(self):
        self.into[self.me] = self.out[self.me]

    def finish(self):
        self.all.wait()


class Total:
    def __init__(self, refs, pair, other, y, y_peers, z, z_peers):
        self.partial, self.pair_in, y_out, y_in, z_out, z_in, sems = refs
        self.pair = pair
        self.swap = remote(self.partial.at[1 - pair], self.pair_in, sems.at[0], sems.at[1], other)
        self.over_y = Exchange(y_out, y_in, sems.at[2], sems.at[3], y, y_peers)
        self.over_z = Exchange(z_out, z_in, sems.at[4], sems.at[5], z, z_peers)

    def start(self):
        self.swap.start()

    def start_y(self):
        self.swap.wait()
        step = self.over_y
        rows = step.out.shape[1]

        def fill(block):
            at = pl.ds(pl.multiple_of(block * rows, 16), rows)
            own = self.partial[self.pair, at, :].astype(F32) + self.pair_in[at, :].astype(F32)
            step.out[block] = own.astype(BF)

        for (block, _), copy in zip(step.peers, step.copies):
            fill(block)
            copy.start()
        fill(step.me)
        step.keep()

    def start_z(self, spread):
        self.over_y.finish()
        rows = jnp.sum(self.over_y.into[...].astype(F32), axis=0).astype(BF)
        step = self.over_z
        planes, out_rows, lanes = step.out.shape
        spaced = dot(spread, rows).reshape(planes, spread.shape[0] // planes, lanes)
        step.out[...] = spaced[:, :out_rows].astype(BF)
        step.start()
        step.keep()

    def finish(self):
        self.over_z.finish()
        return jnp.sum(self.over_z.into[...].astype(F32), axis=0)


def kernel(
    peers,
    heads,
    timesteps,
    ref_losses,
    latent_ref,
    noise_ref,
    weights_hbm,
    grads_out,
    loss_out,
    weights_ref,
    weights_sem,
    input_one,
    qkv_one,
    qkv_two,
    probs_one,
    probs_two,
    attn_one,
    attn_two,
    dout_ref,
    dqkv_ref,
    spare_ref,
    start_pos,
    noise_pos,
    state_ref,
    norm_ref,
    grad_ref,
    sum_out,
    sum_in,
    sum_send,
    sum_recv,
    gather_blocks,
    gather_send,
    gather_recv,
    first_out,
    first_in,
    swap_out,
    swap_in,
    swap_send,
    swap_recv,
    err_x,
    err_x_send,
    err_x_recv,
    err_pair,
    err_pair_send,
    err_pair_recv,
    *total_refs,
):
    pair, seq, x = lax.axis_index("pair"), lax.axis_index("seq"), lax.axis_index("tensor")
    planes = peers // NY
    y, z = seq // planes, seq % planes
    rows, width = latent_ref.shape
    quarter = rows // 4
    tokens = quarter // peers
    half_rows = width // 2
    y_rows = half_rows // NY
    out_rows = y_rows // planes
    z_rows = -(-out_rows // 8) * 8

    def at_x(index):
        return (pair, seq, index)

    def at_y(index):
        return (pair, index * planes + z, x)

    def at_z(index):
        return (pair, y * planes + index, x)

    def at_seq(index):
        return (pair, index, x)

    other = (1 - pair, seq, x)

    columns = weights_hbm.shape[2]
    loads = [
        [
            pltpu.make_async_copy(
                weights_hbm.at[block, slot],
                weights_ref.at[block, pl.ds(slot * LANES, columns)],
                weights_sem.at[block, slot],
            )
            for slot in range(4)
        ]
        for block in range(2)
    ]
    for load in loads[0] + loads[1]:
        load.start()
    for slot in range(4):
        for block in range(2):
            weights_ref[block, slot * LANES + columns : (slot + 1) * LANES, :] = jnp.zeros(
                (LANES - columns, width), BF
            )

    barrier = pltpu.get_barrier_semaphore()

    def greet(offset, carry):
        pl.semaphore_signal(
            barrier, inc=1, device_id=at_seq((seq + offset) % peers), device_id_type=MESH
        )
        return carry

    lax.fori_loop(1, peers, greet, 0)
    for offset in range(1, 4):
        pl.semaphore_signal(
            barrier, inc=1, device_id=at_x((x + offset) % 4), device_id_type=MESH
        )
    pl.semaphore_signal(barrier, inc=1, device_id=other, device_id_type=MESH)

    def hops(offset, count):
        return min(offset, count - offset)

    x_peers = [((x + offset) % 4, at_x((x + offset) % 4)) for offset in (2, 1, 3)]
    y_peers = [((y + offset) % NY, at_y((y + offset) % NY)) for offset in (2, 1, 3)]
    z_order = sorted(range(1, planes), key=lambda offset: -hops(offset, planes))
    z_peers = [((z + offset) % planes, at_z((z + offset) % planes)) for offset in z_order]
    order = sorted(
        ((dy, dz) for dy in range(NY) for dz in range(planes) if dy or dz),
        key=lambda offset: -hops(offset[0], NY) - hops(offset[1], planes),
    )
    seq_peers = []
    for dy, dz in order:
        peer = ((y + dy) % NY) * planes + (z + dz) % planes
        seq_peers.append((peer, at_seq(peer)))

    sums = [
        Exchange(
            sum_out.at[use], sum_in.at[use], sum_send.at[use], sum_recv.at[use], x, x_peers
        )
        for use in range(3)
    ]
    gathers = [
        RingGather(gather_blocks.at[use], gather_send.at[use], gather_recv.at[use], x, at_x)
        for use in range(3)
    ]
    first = Exchange(first_out, first_in, swap_send.at[0], swap_recv.at[0], seq, seq_peers)
    swaps = [
        Exchange(
            swap_out.at[use],
            swap_in.at[use],
            swap_send.at[use + 1],
            swap_recv.at[use + 1],
            seq,
            seq_peers,
        )
        for use in range(2)
    ]
    total_two, total_output, total_queries, total_keys, total_values = [
        Total(total_refs[7 * use : 7 * use + 7], pair, other, y, y_peers, z, z_peers)
        for use in range(5)
    ]

    packing = pack_matrix(peers, tokens)
    unpacking = [unpack_matrix(peers, tokens, third) for third in range(3)]
    time = jnp.full((8, 128), timesteps[0, 0], jnp.int32).astype(F32)
    plan = jnp.cos((time / 1000.0 + 0.008) / 1.008 * (math.pi / 2)) ** 2
    clean_scale = jnp.sqrt(plan)[:1, :1]
    noise_scale = jnp.sqrt(1.0 - plan)[:1, :1]

    state = clean_scale * latent_ref[...].astype(F32) + noise_scale * noise_ref[...].astype(F32)
    center = state - jnp.mean(state, axis=1, keepdims=True)
    inv_std = lax.rsqrt(jnp.mean(center * center, axis=1, keepdims=True) + norm_eps)
    input_one[...] = (center * inv_std).astype(BF)
    for load in loads[0]:
        load.wait()
    qkv_one[...] = dot_nt(input_one[...], weights_ref[0, : 3 * LANES]).astype(BF)
    attend_forward(heads, qkv_one, probs_one, attn_one, None)

    def sum_start(use, rows_ref, weights):
        step = sums[use]
        (opposite, _), (right, _), (left, _) = step.peers
        for blocks in ((opposite, right), (left, x)):
            sources = [
                rows_ref[pl.ds(pl.multiple_of(block * quarter, quarter), quarter), :]
                for block in blocks
            ]
            result = dot(jnp.concatenate(sources, axis=0), weights)
            for place, block in enumerate(blocks):
                step.out[block] = result[place * quarter : (place + 1) * quarter].astype(BF)
            if blocks[0] is opposite:
                step.copies[0].start()
                step.copies[1].start()
            else:
                step.copies[2].start()

    def sum_finish(use):
        step = sums[use]
        step.finish()
        total = step.out[x].astype(F32)
        for peer, _ in step.peers:
            total = total + step.into[peer].astype(F32)
        return total

    pl.semaphore_wait(barrier, peers + 3)
    sum_start(0, attn_one, weights_ref[0, 3 * LANES :])

    mine = pl.ds(pl.multiple_of(x * quarter, quarter), quarter)
    first_out[...] = jnp.concatenate(
        [
            pack(latent_ref[mine, :], packing, peers),
            pack(noise_ref[mine, :], packing, peers),
        ],
        axis=1,
    ).astype(BF)
    first.start()
    first.keep()

    out_one = sum_finish(0)

    swap_out[0] = pack(out_one.astype(BF), packing, peers).astype(BF)
    swaps[0].start()
    swaps[0].keep()
    first.finish()
    messages = first_in[...].astype(F32)
    clean = unpack(messages[:, :8], unpacking, peers)
    noise_pos[...] = unpack(messages[:, 8:], unpacking, peers)
    start_pos[...] = clean_scale * clean + noise_scale * noise_pos[...]
    swaps[0].finish()
    state = start_pos[...] + unpack(swap_in[0].astype(F32), unpacking, peers)
    state_ref[...] = state
    center = state - jnp.mean(state, axis=1, keepdims=True)
    inv_two = lax.rsqrt(jnp.mean(center * center, axis=1, keepdims=True) + norm_eps)
    norm_ref[...] = center * inv_two
    gather_blocks[0, x] = norm_ref[...].astype(BF)
    gathers[0].start()
    gathers[0].middle()

    for load in loads[1]:
        load.wait()
    row, col = iota((rows, 1), 0), iota((1, rows), 1)
    row = row // quarter * tokens + row % tokens
    col = col // quarter * tokens + col % tokens
    same = row == col
    gathers[0].project(weights_ref[1, : 3 * LANES], qkv_two)
    attend_forward(heads, qkv_two, probs_two, attn_two, same)
    sum_start(1, attn_two, weights_ref[1, 3 * LANES :])
    diff = state_ref[...] + sum_finish(1) - noise_pos[...]
    error = jnp.sum(jnp.sum(diff * diff, axis=1, keepdims=True), axis=0, keepdims=True)
    sign = 1.0 - 2.0 * pair.astype(F32)
    grad = diff * (2.0 * sign / width)
    grad_ref[...] = grad
    gather_blocks[1, x] = grad.astype(BF)
    gathers[1].start()
    gathers[1].middle()

    gathers[1].project(weights_ref[1, 3 * LANES :], dout_ref)
    scores_backward(heads, qkv_two, probs_two, dout_ref, dqkv_ref)
    values_backward(heads, probs_two, dout_ref, dqkv_ref)
    sum_start(2, dqkv_ref, weights_ref[1, : 3 * LANES])

    def view(use, start, size):
        return gather_blocks[use, :, :, start : start + size].reshape(rows, size)

    step = 128
    shifted_keys = shifted(dqkv_ref[:, LANES : 2 * LANES], 32)
    shifted_values = shifted(dqkv_ref[:, 2 * LANES :], 64)
    queries_keys = beside(dqkv_ref[:, :LANES].astype(F32), shifted_keys)
    dqkv = jnp.concatenate(
        [
            queries_keys[:, :512],
            queries_keys[:, 512:] + shifted_values[:, :128],
            shifted_values[:, 128:],
        ],
        axis=1,
    ).astype(BF)
    attn = shifted(attn_two[...], 96).astype(BF)
    for start in range(0, width, step):
        first_part = dot_tn(view(0, start, step), dqkv)
        second_part = dot_tn(view(1, start, step), attn)
        block = jnp.concatenate(
            [
                first_part[:, :768],
                first_part[:, 768:] + second_part[:, :128],
                second_part[:, 128:],
            ],
            axis=1,
        )
        store_rows(total_two.partial, start, block, half_rows)
    total_two.start()
    dnorm = sum_finish(2)
    normed = norm_ref[...]
    mean_grad = jnp.mean(dnorm, axis=1, keepdims=True)
    mean_prod = jnp.mean(dnorm * normed, axis=1, keepdims=True)
    dstate = grad_ref[...] + inv_two * (dnorm - mean_grad - normed * mean_prod)

    messages = pack(dstate.astype(BF), packing, peers)
    inner = iota(messages.shape, 1)
    error_high = error.astype(BF).astype(F32)
    error_low = error - error_high
    messages = jnp.where(inner == 6, error_high.reshape(1, 1, 1), messages)
    messages = jnp.where(inner == 7, error_low.reshape(1, 1, 1), messages)
    swap_out[1] = messages.astype(BF)
    swaps[1].start()
    swaps[1].keep()

    row = iota((planes * z_rows, 1), 0)
    inner = row % z_rows
    source = jnp.where(inner < out_rows, (row // z_rows) * out_rows + inner, -1)
    spread = selection(source, y_rows)

    total_two.start_y()
    swaps[1].finish()
    messages = swap_in[1].astype(F32)
    gather_blocks[2, x] = unpack(messages, unpacking, peers).astype(BF)
    gathers[2].start()
    total = jnp.sum(messages, axis=0)
    err_x[x] = jnp.broadcast_to(total[6:7, :128] + total[7:8, :128], (8, 128))
    err_copies = [
        remote(
            err_x.at[x],
            err_x.at[x],
            err_x_send.at[offset - 1],
            err_x_recv.at[offset - 1],
            at_x((x + offset) % 4),
        )
        for offset in range(1, 4)
    ]
    for copy in err_copies:
        copy.start()
    gathers[2].middle()

    gathers[2].project(weights_ref[0, 3 * LANES :], dout_ref)
    for start in range(0, width, step):
        block = dot_tn(view(2, start, step), attn_one[...])
        store_rows(total_output.partial, start, block[:, :256], half_rows)
        spare_ref[start : start + step, :] = pltpu.roll(block[:, 256:], 64, 1)
    total_output.start()
    scores_backward(heads, qkv_one, probs_one, dout_ref, dqkv_ref)
    total_output.start_y()
    values_backward(heads, probs_one, dout_ref, dqkv_ref)
    queries_keys = beside(
        dqkv_ref[:, :LANES].astype(F32), shifted(dqkv_ref[:, LANES : 2 * LANES], 32)
    )
    spare = shifted(dqkv_ref[:, 2 * LANES + 256 :], 96)
    operand = jnp.concatenate(
        [queries_keys[:, :512], queries_keys[:, 512:] + spare], axis=1
    ).astype(BF)
    for start in range(0, width, step):
        block = dot_tn(input_one[:, start : start + step], operand)
        last = block[:, 512:] + spare_ref[start : start + step, :]
        store_rows(total_queries.partial, start, block[:, :LANES], half_rows)
        store_rows(
            total_keys.partial,
            start,
            jnp.concatenate([block[:, LANES:512], last], axis=1),
            half_rows,
        )
    total_queries.start()
    total_keys.start()
    total_two.start_z(spread)
    total_queries.start_y()
    total_keys.start_y()
    for start in range(0, width, step):
        block = dot_tn(input_one[:, start : start + step], dqkv_ref[:, 2 * LANES : 2 * LANES + 256])
        store_rows(total_values.partial, start, block, half_rows)
    total_values.start()
    for copy in err_copies:
        copy.wait()
    err_pair[pair] = jnp.sum(err_x[...], axis=0)
    err_copy = remote(err_pair.at[pair], err_pair.at[pair], err_pair_send, err_pair_recv, other)
    err_copy.start()
    total_values.start_y()
    total_output.start_z(spread)
    err_copy.wait()
    margin = (err_pair[0] - err_pair[1]) * (1.0 / (rows * peers * width))
    scaled = beta_dpo * (margin - (ref_losses[0] - ref_losses[1]))
    loss = jnp.maximum(scaled, 0.0) + jnp.log1p(jnp.exp(-jnp.abs(scaled)))
    loss_out[0, 0] = loss[0, 0]
    factor = (rows * peers * beta_dpo) * jax.nn.sigmoid(scaled)
    factor = factor[:1, :1]
    total_queries.start_z(spread)
    total_keys.start_z(spread)
    total_values.start_z(spread)
    grads_out[:, 1, :] = total_two.finish() * factor
    empty = jnp.zeros((out_rows, 128), F32)
    output = pltpu.roll(jnp.concatenate([total_output.finish(), empty], axis=1), 96, 1)
    queries = total_queries.finish()
    keys = total_keys.finish()
    values = pltpu.roll(jnp.concatenate([total_values.finish(), empty], axis=1), 64, 1)
    last = keys[:, 128:]
    lane = iota((1, 128), 1)
    values_rest = jnp.where((lane >= 64) & (lane < 96), pltpu.roll(last, 96, 1), 0.0)
    output_rest = jnp.where(lane >= 96, pltpu.roll(last, 32, 1), 0.0)
    grads = jnp.concatenate(
        [
            queries,
            keys[:, :128],
            jnp.where(lane < 64, last, 0.0) + values[:, :128],
            values[:, 128:256],
            values[:, 256:] + output[:, :128] + values_rest,
            output[:, 128:256],
            output[:, 256:] + output_rest,
        ],
        axis=1,
    )
    grads_out[:, 0, :] = grads * factor


def local(latents, noise, timesteps, ref_losses, weights):
    width, columns = weights.shape[0], weights.shape[3]
    rows = latents.shape[2]
    peers = lax.axis_size("seq")
    quarter = rows // 4
    planes = peers // NY
    half_rows = width // 2
    y_rows = half_rows // NY
    out_rows = y_rows // planes
    heads = columns // HEAD_DIM

    vmem = pltpu.VMEM
    dma = pltpu.SemaphoreType.DMA
    third = width // 3
    totals = []
    for lanes in (width, 256, LANES, 256, 256):
        totals += [
            vmem((2, half_rows, lanes), BF),
            vmem((half_rows, lanes), BF),
            vmem((NY, y_rows, lanes), BF),
            vmem((NY, y_rows, lanes), BF),
            vmem((planes, out_rows, lanes), BF),
            vmem((planes, out_rows, lanes), BF),
            dma((6,)),
        ]
    grads, loss = pl.pallas_call(
        functools.partial(kernel, peers, heads),
        out_shape=(
            jax.ShapeDtypeStruct((out_rows, 2, width), F32),
            jax.ShapeDtypeStruct((1, 1), F32),
        ),
        in_specs=[
            pl.BlockSpec(memory_space=pltpu.SMEM),
            pl.BlockSpec(memory_space=pltpu.SMEM),
            pl.BlockSpec(memory_space=vmem),
            pl.BlockSpec(memory_space=vmem),
            pl.BlockSpec(memory_space=pl.ANY),
        ],
        out_specs=(pl.BlockSpec(memory_space=vmem), pl.BlockSpec(memory_space=pltpu.SMEM)),
        scratch_shapes=[
            vmem((2, 4 * LANES, width), BF),
            dma((2, 4)),
            vmem((rows, width), BF),
            vmem((rows, 3 * LANES), BF),
            vmem((rows, 3 * LANES), BF),
            vmem((heads, rows, rows), F32),
            vmem((heads, rows, rows), F32),
            vmem((rows, LANES), BF),
            vmem((rows, LANES), BF),
            vmem((rows, LANES), BF),
            vmem((rows, 3 * LANES), BF),
            vmem((width, 128), F32),
            vmem((quarter, width), F32),
            vmem((quarter, width), F32),
            vmem((quarter, width), F32),
            vmem((quarter, width), F32),
            vmem((quarter, width), F32),
            vmem((3, 4, quarter, width), BF),
            vmem((3, 4, quarter, width), BF),
            dma((3,)),
            dma((3,)),
            vmem((3, 4, quarter, width), BF),
            dma((3, 10)),
            dma((3, 10)),
            vmem((peers, 16, third), BF),
            vmem((peers, 16, third), BF),
            vmem((2, peers, 8, third), BF),
            vmem((2, peers, 8, third), BF),
            dma((3,)),
            dma((3,)),
            vmem((4, 8, 128), F32),
            dma((3,)),
            dma((3,)),
            vmem((2, 8, 128), F32),
            dma,
            dma,
            *totals,
        ],
        compiler_params=pltpu.CompilerParams(
            collective_id=0, has_side_effects=True, vmem_limit_bytes=60 * 2**20
        ),
    )(timesteps, ref_losses[:, 0], latents[0, 0], noise[0, 0], weights.transpose(1, 2, 3, 0))

    return (loss[0, 0], grads.reshape(out_rows, 2, 4, columns))


def solution(mesh):
    in_specs = (
        P("pair", None, "seq", None),
        P("pair", None, "seq", None),
        P("pair", None),
        P(),
        P(None, None, None, "tensor"),
    )
    out_specs = (P(), P(("pair", "seq"), None, None, "tensor"))
    return jax.shard_map(local, mesh=mesh, in_specs=in_specs, out_specs=out_specs, check_vma=False)
```

```python
import functools
import math

import jax
import jax.numpy as jnp
from jax import lax
from jax.experimental import pallas as pl
from jax.experimental.pallas import tpu as pltpu
from jax.sharding import PartitionSpec as P

HEAD_DIM = 72
LANES = 384
NY = 4
MESH = pl.DeviceIdType.MESH
BF = jnp.bfloat16
F32 = jnp.float32

beta_dpo = 0.5
norm_eps = 1e-06


def dot(a, b):
    return jnp.dot(a, b, preferred_element_type=F32)


def dot_nt(a, b):
    return lax.dot_general(a, b, (((1,), (1,)), ((), ())), preferred_element_type=F32)


def dot_tn(a, b):
    return lax.dot_general(a, b, (((0,), (0,)), ((), ())), preferred_element_type=F32)


def iota(shape, axis):
    return lax.broadcasted_iota(jnp.int32, shape, axis)


def head_mask(head, dtype):
    lane = iota((1, LANES), 1)
    return ((lane >= head * HEAD_DIM) & (lane < (head + 1) * HEAD_DIM)).astype(dtype)


def attend_forward(heads, qkv_ref, probs_ref, out_ref, mask):
    queries = qkv_ref[:, :LANES]
    keys = qkv_ref[:, LANES : 2 * LANES]
    values = qkv_ref[:, 2 * LANES :]
    total = None
    for head in range(heads):
        scores = dot_nt(queries * head_mask(head, BF), keys) * (HEAD_DIM**-0.5)
        if mask is not None:
            scores = jnp.where(mask, scores, -1e30)
        scores = jnp.exp(scores - jnp.max(scores, axis=1, keepdims=True))
        probs = scores * (1.0 / jnp.sum(scores, axis=1, keepdims=True))
        probs_ref[head] = probs
        part = dot(probs.astype(BF), values) * head_mask(head, F32)
        total = part if total is None else total + part
    out_ref[...] = total.astype(BF)


def values_backward(heads, probs_ref, grad_ref, dqkv_ref):
    grad = grad_ref[...]
    total = None
    for head in range(heads):
        part = dot_tn(probs_ref[head].astype(BF), grad) * head_mask(head, F32)
        total = part if total is None else total + part
    dqkv_ref[:, 2 * LANES :] = total.astype(BF)


def scores_backward(heads, qkv_ref, probs_ref, grad_ref, dqkv_ref):
    queries = qkv_ref[:, :LANES]
    keys = qkv_ref[:, LANES : 2 * LANES]
    values = qkv_ref[:, 2 * LANES :]
    grad = grad_ref[...]
    sums = [None, None]
    for head in range(heads):
        probs = probs_ref[head]
        dprobs = dot_nt(grad * head_mask(head, BF), values)
        delta = jnp.sum(dprobs * probs, axis=1, keepdims=True)
        dscores = (probs * (dprobs - delta) * (HEAD_DIM**-0.5)).astype(BF)
        parts = (dot(dscores, keys), dot_tn(dscores, queries))
        for slot in range(2):
            part = parts[slot] * head_mask(head, F32)
            sums[slot] = part if sums[slot] is None else sums[slot] + part
    for slot in range(2):
        dqkv_ref[:, slot * LANES : (slot + 1) * LANES] = sums[slot].astype(BF)


def beside(first, second):
    return jnp.concatenate(
        [first[:, :256], first[:, 256:] + second[:, :128], second[:, 128:]], axis=1
    )


def shifted(values, lanes):
    return pltpu.roll(values.astype(F32), lanes, 1)


def store_rows(out_ref, start, rows, half_rows):
    done, count = 0, rows.shape[0]
    while done < count:
        half, at = divmod(start + done, half_rows)
        size = min(count - done, half_rows - at)
        out_ref[half, at : at + size, :] = rows[done : done + size].astype(BF)
        done += size


def selection(source, columns):
    col = iota((source.shape[0], columns), 1)
    return (col == source).astype(F32).astype(BF)


def pack_matrix(peers, tokens):
    row = iota((8 * peers, 1), 0)
    peer, inner = row // 8, row % 8
    source = (inner // tokens) * (peers * tokens) + peer * tokens + inner % tokens
    return selection(jnp.where(inner < 3 * tokens, source, -1), 3 * peers * tokens)


def unpack_matrix(peers, tokens, third):
    token = iota((peers * tokens, 1), 0)
    source = (token // tokens) * 8 + third * tokens + token % tokens
    return selection(source, 8 * peers)


def pack(rows, matrix, peers):
    third = rows.shape[1] // 3
    stacked = jnp.concatenate(
        [rows[:, :third], rows[:, third : 2 * third], rows[:, 2 * third :]], axis=0
    )
    return dot(matrix, stacked).reshape(peers, 8, third)


def unpack(messages, matrices, peers):
    flat = messages.reshape(8 * peers, messages.shape[2]).astype(BF)
    return jnp.concatenate([dot(matrix, flat) for matrix in matrices], axis=1)


def remote(src, dst, send, recv, device):
    return pltpu.make_async_remote_copy(
        src_ref=src,
        dst_ref=dst,
        send_sem=send,
        recv_sem=recv,
        device_id=device,
        device_id_type=MESH,
    )


def halves(rows):
    unit = 16 if rows >= 64 else rows // 4
    cut = -(-rows // (2 * unit)) * unit
    low, high = -(-cut // (2 * unit)) * unit, -(-(rows - cut) // (2 * unit)) * unit
    return (
        cut,
        ((0, low), (low, cut - low)),
        ((cut, high), (cut + high, rows - cut - high)),
    )


class RingGather:
    def __init__(self, blocks, send, recv, me, device):
        self.blocks, self.me = blocks, me
        self.right, self.left = (me + 1) % 4, (me + 3) % 4
        self.opposite = (me + 2) % 4
        rows = blocks.shape[1]
        cut, lows, highs = halves(rows)
        right, left = device(self.right), device(self.left)

        def copy(block, piece, index, to):
            ref = blocks.at[block, pl.ds(*piece)]
            return remote(ref, ref, send.at[index], recv.at[index], to)

        self.first, self.passes = [], []
        for place, piece in enumerate(lows):
            self.first.append(copy(me, piece, place, right))
            self.passes.append(copy(self.left, piece, 4 + place, right))
        for place, piece in enumerate(highs):
            self.first.append(copy(me, piece, 2 + place, left))
            self.passes.append(copy(self.right, piece, 6 + place, left))
        self.next_right = copy(me, (cut, rows - cut), 8, right)
        self.next_left = copy(me, (0, cut), 9, left)

    def start(self):
        for place in (0, 2, 1, 3):
            self.first[place].start()
        self.next_right.start()
        self.next_left.start()

    def middle(self):
        for place in (0, 2, 1, 3):
            self.first[place].wait_recv()
            self.passes[place].start()

    def project(self, weights, out_ref):
        size = self.blocks.shape[1]
        self.next_right.wait_recv()
        self.next_left.wait_recv()
        near = (self.me, self.left, self.right)
        result = dot_nt(jnp.concatenate([self.blocks[block] for block in near], axis=0), weights)
        for place, block in enumerate(near):
            out_ref[pl.ds(pl.multiple_of(block * size, size), size), :] = result[
                place * size : (place + 1) * size
            ].astype(BF)
        for copy in self.passes:
            copy.wait_recv()
        out_ref[pl.ds(pl.multiple_of(self.opposite * size, size), size), :] = dot_nt(
            self.blocks[self.opposite], weights
        ).astype(BF)
        for copy in self.first + self.passes + [self.next_right, self.next_left]:
            copy.wait_send()


class Exchange:
    def __init__(self, out, into, send, recv, me, peers):
        self.out, self.into, self.me, self.peers = out, into, me, peers
        self.copies = [
            remote(out.at[peer], into.at[me], send, recv, device) for peer, device in peers
        ]
        every = pl.ds(0, len(peers))
        self.all = remote(out.at[every], into.at[every], send, recv, peers[0][1])

    def start(self):
        for copy in self.copies:
            copy.start()

    def keep(self):
        self.into[self.me] = self.out[self.me]

    def finish(self):
        self.all.wait()


class Total:
    def __init__(self, refs, pair, other, y, y_peers, z, z_peers):
        self.partial, self.pair_in, y_out, y_in, z_out, z_in, sems = refs
        self.pair = pair
        self.swap = remote(self.partial.at[1 - pair], self.pair_in, sems.at[0], sems.at[1], other)
        self.over_y = Exchange(y_out, y_in, sems.at[2], sems.at[3], y, y_peers)
        self.over_z = Exchange(z_out, z_in, sems.at[4], sems.at[5], z, z_peers)

    def start(self):
        self.swap.start()

    def start_y(self):
        self.swap.wait()
        step = self.over_y
        rows = step.out.shape[1]

        def fill(block):
            at = pl.ds(pl.multiple_of(block * rows, 16), rows)
            own = self.partial[self.pair, at, :].astype(F32) + self.pair_in[at, :].astype(F32)
            step.out[block] = own.astype(BF)

        for (block, _), copy in zip(step.peers, step.copies):
            fill(block)
            copy.start()
        fill(step.me)
        step.keep()

    def start_z(self, spread):
        self.over_y.finish()
        rows = jnp.sum(self.over_y.into[...].astype(F32), axis=0).astype(BF)
        step = self.over_z
        planes, out_rows, lanes = step.out.shape
        spaced = dot(spread, rows).reshape(planes, spread.shape[0] // planes, lanes)
        step.out[...] = spaced[:, :out_rows].astype(BF)
        step.start()
        step.keep()

    def finish(self):
        self.over_z.finish()
        return jnp.sum(self.over_z.into[...].astype(F32), axis=0)


def kernel(
    peers,
    heads,
    timesteps,
    ref_losses,
    latent_ref,
    noise_ref,
    weights_hbm,
    grads_out,
    loss_out,
    weights_ref,
    weights_sem,
    input_one,
    qkv_one,
    qkv_two,
    probs_one,
    probs_two,
    attn_one,
    attn_two,
    dout_ref,
    dqkv_ref,
    spare_ref,
    start_pos,
    noise_pos,
    state_ref,
    norm_ref,
    grad_ref,
    sum_out,
    sum_in,
    sum_send,
    sum_recv,
    gather_blocks,
    gather_send,
    gather_recv,
    first_out,
    first_in,
    swap_out,
    swap_in,
    swap_send,
    swap_recv,
    err_x,
    err_x_send,
    err_x_recv,
    err_pair,
    err_pair_send,
    err_pair_recv,
    *total_refs,
):
    pair, seq, x = lax.axis_index("pair"), lax.axis_index("seq"), lax.axis_index("tensor")
    planes = peers // NY
    y, z = seq // planes, seq % planes
    rows, width = latent_ref.shape
    quarter = rows // 4
    tokens = quarter // peers
    half_rows = width // 2
    y_rows = half_rows // NY
    out_rows = y_rows // planes
    z_rows = -(-out_rows // 8) * 8

    def at_x(index):
        return (pair, seq, index)

    def at_y(index):
        return (pair, index * planes + z, x)

    def at_z(index):
        return (pair, y * planes + index, x)

    def at_seq(index):
        return (pair, index, x)

    other = (1 - pair, seq, x)

    columns = weights_hbm.shape[2]
    loads = [
        [
            pltpu.make_async_copy(
                weights_hbm.at[block, slot],
                weights_ref.at[block, pl.ds(slot * LANES, columns)],
                weights_sem.at[block, slot],
            )
            for slot in range(4)
        ]
        for block in range(2)
    ]
    for load in loads[0] + loads[1]:
        load.start()
    for slot in range(4):
        for block in range(2):
            weights_ref[block, slot * LANES + columns : (slot + 1) * LANES, :] = jnp.zeros(
                (LANES - columns, width), BF
            )

    barrier = pltpu.get_barrier_semaphore()

    def greet(offset, carry):
        pl.semaphore_signal(
            barrier, inc=1, device_id=at_seq((seq + offset) % peers), device_id_type=MESH
        )
        return carry

    lax.fori_loop(1, peers, greet, 0)
    for offset in range(1, 4):
        pl.semaphore_signal(
            barrier, inc=1, device_id=at_x((x + offset) % 4), device_id_type=MESH
        )
    pl.semaphore_signal(barrier, inc=1, device_id=other, device_id_type=MESH)

    def hops(offset, count):
        return min(offset, count - offset)

    x_peers = [((x + offset) % 4, at_x((x + offset) % 4)) for offset in (2, 1, 3)]
    y_peers = [((y + offset) % NY, at_y((y + offset) % NY)) for offset in (2, 1, 3)]
    z_order = sorted(range(1, planes), key=lambda offset: -hops(offset, planes))
    z_peers = [((z + offset) % planes, at_z((z + offset) % planes)) for offset in z_order]
    order = sorted(
        ((dy, dz) for dy in range(NY) for dz in range(planes) if dy or dz),
        key=lambda offset: -hops(offset[0], NY) - hops(offset[1], planes),
    )
    seq_peers = []
    for dy, dz in order:
        peer = ((y + dy) % NY) * planes + (z + dz) % planes
        seq_peers.append((peer, at_seq(peer)))

    sums = [
        Exchange(
            sum_out.at[use], sum_in.at[use], sum_send.at[use], sum_recv.at[use], x, x_peers
        )
        for use in range(3)
    ]
    gathers = [
        RingGather(gather_blocks.at[use], gather_send.at[use], gather_recv.at[use], x, at_x)
        for use in range(3)
    ]
    first = Exchange(first_out, first_in, swap_send.at[0], swap_recv.at[0], seq, seq_peers)
    swaps = [
        Exchange(
            swap_out.at[use],
            swap_in.at[use],
            swap_send.at[use + 1],
            swap_recv.at[use + 1],
            seq,
            seq_peers,
        )
        for use in range(2)
    ]
    total_two, total_output, total_queries, total_keys, total_values = [
        Total(total_refs[7 * use : 7 * use + 7], pair, other, y, y_peers, z, z_peers)
        for use in range(5)
    ]

    packing = pack_matrix(peers, tokens)
    unpacking = [unpack_matrix(peers, tokens, third) for third in range(3)]
    time = jnp.full((8, 128), timesteps[0, 0], jnp.int32).astype(F32)
    plan = jnp.cos((time / 1000.0 + 0.008) / 1.008 * (math.pi / 2)) ** 2
    clean_scale = jnp.sqrt(plan)[:1, :1]
    noise_scale = jnp.sqrt(1.0 - plan)[:1, :1]

    state = clean_scale * latent_ref[...].astype(F32) + noise_scale * noise_ref[...].astype(F32)
    center = state - jnp.mean(state, axis=1, keepdims=True)
    inv_std = lax.rsqrt(jnp.mean(center * center, axis=1, keepdims=True) + norm_eps)
    input_one[...] = (center * inv_std).astype(BF)
    for load in loads[0]:
        load.wait()
    qkv_one[...] = dot_nt(input_one[...], weights_ref[0, : 3 * LANES]).astype(BF)
    attend_forward(heads, qkv_one, probs_one, attn_one, None)

    def sum_start(use, rows_ref, weights):
        step = sums[use]
        (opposite, _), (right, _), (left, _) = step.peers
        for blocks in ((opposite, right), (left, x)):
            sources = [
                rows_ref[pl.ds(pl.multiple_of(block * quarter, quarter), quarter), :]
                for block in blocks
            ]
            result = dot(jnp.concatenate(sources, axis=0), weights)
            for place, block in enumerate(blocks):
                step.out[block] = result[place * quarter : (place + 1) * quarter].astype(BF)
            if blocks[0] is opposite:
                step.copies[0].start()
                step.copies[1].start()
            else:
                step.copies[2].start()

    def sum_finish(use):
        step = sums[use]
        step.finish()
        total = step.out[x].astype(F32)
        for peer, _ in step.peers:
            total = total + step.into[peer].astype(F32)
        return total

    pl.semaphore_wait(barrier, peers + 3)
    sum_start(0, attn_one, weights_ref[0, 3 * LANES :])

    mine = pl.ds(pl.multiple_of(x * quarter, quarter), quarter)
    first_out[...] = jnp.concatenate(
        [
            pack(latent_ref[mine, :], packing, peers),
            pack(noise_ref[mine, :], packing, peers),
        ],
        axis=1,
    ).astype(BF)
    first.start()
    first.keep()

    out_one = sum_finish(0)

    swap_out[0] = pack(out_one.astype(BF), packing, peers).astype(BF)
    swaps[0].start()
    swaps[0].keep()
    first.finish()
    messages = first_in[...].astype(F32)
    clean = unpack(messages[:, :8], unpacking, peers)
    noise_pos[...] = unpack(messages[:, 8:], unpacking, peers)
    start_pos[...] = clean_scale * clean + noise_scale * noise_pos[...]
    swaps[0].finish()
    state = start_pos[...] + unpack(swap_in[0].astype(F32), unpacking, peers)
    state_ref[...] = state
    center = state - jnp.mean(state, axis=1, keepdims=True)
    inv_two = lax.rsqrt(jnp.mean(center * center, axis=1, keepdims=True) + norm_eps)
    norm_ref[...] = center * inv_two
    gather_blocks[0, x] = norm_ref[...].astype(BF)
    gathers[0].start()
    gathers[0].middle()

    for load in loads[1]:
        load.wait()
    row, col = iota((rows, 1), 0), iota((1, rows), 1)
    row = row // quarter * tokens + row % tokens
    col = col // quarter * tokens + col % tokens
    same = row == col
    gathers[0].project(weights_ref[1, : 3 * LANES], qkv_two)
    attend_forward(heads, qkv_two, probs_two, attn_two, same)
    sum_start(1, attn_two, weights_ref[1, 3 * LANES :])
    diff = state_ref[...] + sum_finish(1) - noise_pos[...]
    error = jnp.sum(jnp.sum(diff * diff, axis=1, keepdims=True), axis=0, keepdims=True)
    sign = 1.0 - 2.0 * pair.astype(F32)
    grad = diff * (2.0 * sign / width)
    grad_ref[...] = grad
    gather_blocks[1, x] = grad.astype(BF)
    gathers[1].start()
    gathers[1].middle()

    gathers[1].project(weights_ref[1, 3 * LANES :], dout_ref)
    scores_backward(heads, qkv_two, probs_two, dout_ref, dqkv_ref)
    values_backward(heads, probs_two, dout_ref, dqkv_ref)
    sum_start(2, dqkv_ref, weights_ref[1, : 3 * LANES])

    def view(use, start, size):
        return gather_blocks[use, :, :, start : start + size].reshape(rows, size)

    step = 128
    shifted_keys = shifted(dqkv_ref[:, LANES : 2 * LANES], 32)
    shifted_values = shifted(dqkv_ref[:, 2 * LANES :], 64)
    queries_keys = beside(dqkv_ref[:, :LANES].astype(F32), shifted_keys)
    dqkv = jnp.concatenate(
        [
            queries_keys[:, :512],
            queries_keys[:, 512:] + shifted_values[:, :128],
            shifted_values[:, 128:],
        ],
        axis=1,
    ).astype(BF)
    attn = shifted(attn_two[...], 96).astype(BF)
    for start in range(0, width, step):
        first_part = dot_tn(view(0, start, step), dqkv)
        second_part = dot_tn(view(1, start, step), attn)
        block = jnp.concatenate(
            [
                first_part[:, :768],
                first_part[:, 768:] + second_part[:, :128],
                second_part[:, 128:],
            ],
            axis=1,
        )
        store_rows(total_two.partial, start, block, half_rows)
    total_two.start()
    dnorm = sum_finish(2)
    normed = norm_ref[...]
    mean_grad = jnp.mean(dnorm, axis=1, keepdims=True)
    mean_prod = jnp.mean(dnorm * normed, axis=1, keepdims=True)
    dstate = grad_ref[...] + inv_two * (dnorm - mean_grad - normed * mean_prod)

    messages = pack(dstate.astype(BF), packing, peers)
    inner = iota(messages.shape, 1)
    error_high = error.astype(BF).astype(F32)
    error_low = error - error_high
    messages = jnp.where(inner == 6, error_high.reshape(1, 1, 1), messages)
    messages = jnp.where(inner == 7, error_low.reshape(1, 1, 1), messages)
    swap_out[1] = messages.astype(BF)
    swaps[1].start()
    swaps[1].keep()

    row = iota((planes * z_rows, 1), 0)
    inner = row % z_rows
    source = jnp.where(inner < out_rows, (row // z_rows) * out_rows + inner, -1)
    spread = selection(source, y_rows)

    total_two.start_y()
    swaps[1].finish()
    messages = swap_in[1].astype(F32)
    gather_blocks[2, x] = unpack(messages, unpacking, peers).astype(BF)
    gathers[2].start()
    total = jnp.sum(messages, axis=0)
    err_x[x] = jnp.broadcast_to(total[6:7, :128] + total[7:8, :128], (8, 128))
    err_copies = [
        remote(
            err_x.at[x],
            err_x.at[x],
            err_x_send.at[offset - 1],
            err_x_recv.at[offset - 1],
            at_x((x + offset) % 4),
        )
        for offset in range(1, 4)
    ]
    for copy in err_copies:
        copy.start()
    gathers[2].middle()

    gathers[2].project(weights_ref[0, 3 * LANES :], dout_ref)
    for start in range(0, width, step):
        block = dot_tn(view(2, start, step), attn_one[...])
        store_rows(total_output.partial, start, block[:, :256], half_rows)
        spare_ref[start : start + step, :] = pltpu.roll(block[:, 256:], 64, 1)
    total_output.start()
    values_backward(heads, probs_one, dout_ref, dqkv_ref)
    for start in range(0, width, step):
        block = dot_tn(
            input_one[:, start : start + step], dqkv_ref[:, 2 * LANES : 2 * LANES + 256]
        )
        store_rows(total_values.partial, start, block, half_rows)
    total_values.start()
    total_output.start_y()
    total_two.start_z(spread)
    scores_backward(heads, qkv_one, probs_one, dout_ref, dqkv_ref)
    total_values.start_y()
    queries_keys = beside(
        dqkv_ref[:, :LANES].astype(F32), shifted(dqkv_ref[:, LANES : 2 * LANES], 32)
    )
    spare = shifted(dqkv_ref[:, 2 * LANES + 256 :], 96)
    operand = queries_keys[:, :LANES].astype(BF)
    for start in range(0, width, step):
        block = dot_tn(input_one[:, start : start + step], operand)
        store_rows(total_queries.partial, start, block, half_rows)
    total_queries.start()
    operand = jnp.concatenate(
        [queries_keys[:, LANES:512], queries_keys[:, 512:] + spare], axis=1
    ).astype(BF)
    for start in range(0, width, step):
        block = dot_tn(input_one[:, start : start + step], operand)
        last = block[:, 128:] + spare_ref[start : start + step, :]
        block = jnp.concatenate([block[:, :128], last], axis=1)
        store_rows(total_keys.partial, start, block, half_rows)
    total_keys.start()
    total_queries.start_y()
    total_keys.start_y()
    for copy in err_copies:
        copy.wait()
    err_pair[pair] = jnp.sum(err_x[...], axis=0)
    err_copy = remote(err_pair.at[pair], err_pair.at[pair], err_pair_send, err_pair_recv, other)
    err_copy.start()
    total_output.start_z(spread)
    total_values.start_z(spread)
    err_copy.wait()
    margin = (err_pair[0] - err_pair[1]) * (1.0 / (rows * peers * width))
    scaled = beta_dpo * (margin - (ref_losses[0] - ref_losses[1]))
    loss = jnp.maximum(scaled, 0.0) + jnp.log1p(jnp.exp(-jnp.abs(scaled)))
    loss_out[0, 0] = loss[0, 0]
    factor = (rows * peers * beta_dpo) * jax.nn.sigmoid(scaled)
    factor = factor[:1, :1]
    total_queries.start_z(spread)
    total_keys.start_z(spread)
    grads_out[:, 1, :] = total_two.finish() * factor
    empty = jnp.zeros((out_rows, 128), F32)
    output = pltpu.roll(jnp.concatenate([total_output.finish(), empty], axis=1), 96, 1)
    queries = total_queries.finish()
    keys = total_keys.finish()
    values = pltpu.roll(jnp.concatenate([total_values.finish(), empty], axis=1), 64, 1)
    last = keys[:, 128:]
    lane = iota((1, 128), 1)
    values_rest = jnp.where((lane >= 64) & (lane < 96), pltpu.roll(last, 96, 1), 0.0)
    output_rest = jnp.where(lane >= 96, pltpu.roll(last, 32, 1), 0.0)
    grads = jnp.concatenate(
        [
            queries,
            keys[:, :128],
            jnp.where(lane < 64, last, 0.0) + values[:, :128],
            values[:, 128:256],
            values[:, 256:] + output[:, :128] + values_rest,
            output[:, 128:256],
            output[:, 256:] + output_rest,
        ],
        axis=1,
    )
    grads_out[:, 0, :] = grads * factor


def local(latents, noise, timesteps, ref_losses, weights):
    width, columns = weights.shape[0], weights.shape[3]
    rows = latents.shape[2]
    peers = lax.axis_size("seq")
    quarter = rows // 4
    planes = peers // NY
    half_rows = width // 2
    y_rows = half_rows // NY
    out_rows = y_rows // planes
    heads = columns // HEAD_DIM

    vmem = pltpu.VMEM
    dma = pltpu.SemaphoreType.DMA
    third = width // 3
    totals = []
    for lanes in (width, 256, LANES, 256, 256):
        totals += [
            vmem((2, half_rows, lanes), BF),
            vmem((half_rows, lanes), BF),
            vmem((NY, y_rows, lanes), BF),
            vmem((NY, y_rows, lanes), BF),
            vmem((planes, out_rows, lanes), BF),
            vmem((planes, out_rows, lanes), BF),
            dma((6,)),
        ]
    grads, loss = pl.pallas_call(
        functools.partial(kernel, peers, heads),
        out_shape=(
            jax.ShapeDtypeStruct((out_rows, 2, width), F32),
            jax.ShapeDtypeStruct((1, 1), F32),
        ),
        in_specs=[
            pl.BlockSpec(memory_space=pltpu.SMEM),
            pl.BlockSpec(memory_space=pltpu.SMEM),
            pl.BlockSpec(memory_space=vmem),
            pl.BlockSpec(memory_space=vmem),
            pl.BlockSpec(memory_space=pl.ANY),
        ],
        out_specs=(pl.BlockSpec(memory_space=vmem), pl.BlockSpec(memory_space=pltpu.SMEM)),
        scratch_shapes=[
            vmem((2, 4 * LANES, width), BF),
            dma((2, 4)),
            vmem((rows, width), BF),
            vmem((rows, 3 * LANES), BF),
            vmem((rows, 3 * LANES), BF),
            vmem((heads, rows, rows), F32),
            vmem((heads, rows, rows), F32),
            vmem((rows, LANES), BF),
            vmem((rows, LANES), BF),
            vmem((rows, LANES), BF),
            vmem((rows, 3 * LANES), BF),
            vmem((width, 128), F32),
            vmem((quarter, width), F32),
            vmem((quarter, width), F32),
            vmem((quarter, width), F32),
            vmem((quarter, width), F32),
            vmem((quarter, width), F32),
            vmem((3, 4, quarter, width), BF),
            vmem((3, 4, quarter, width), BF),
            dma((3,)),
            dma((3,)),
            vmem((3, 4, quarter, width), BF),
            dma((3, 10)),
            dma((3, 10)),
            vmem((peers, 16, third), BF),
            vmem((peers, 16, third), BF),
            vmem((2, peers, 8, third), BF),
            vmem((2, peers, 8, third), BF),
            dma((3,)),
            dma((3,)),
            vmem((4, 8, 128), F32),
            dma((3,)),
            dma((3,)),
            vmem((2, 8, 128), F32),
            dma,
            dma,
            *totals,
        ],
        compiler_params=pltpu.CompilerParams(
            collective_id=0, has_side_effects=True, vmem_limit_bytes=60 * 2**20
        ),
    )(timesteps, ref_losses[:, 0], latents[0, 0], noise[0, 0], weights.transpose(1, 2, 3, 0))

    return (loss[0, 0], grads.reshape(out_rows, 2, 4, columns))


def solution(mesh):
    in_specs = (
        P("pair", None, "seq", None),
        P("pair", None, "seq", None),
        P("pair", None),
        P(),
        P(None, None, None, "tensor"),
    )
    out_specs = (P(), P(("pair", "seq"), None, None, "tensor"))
    return jax.shard_map(local, mesh=mesh, in_specs=in_specs, out_specs=out_specs, check_vma=False)
```
